512 devices in a mesh: seq: 16 (over y, x_hi, core), exp: 32 (over z, x_lo).
Axes of the slice: x: 4 (x_hi: 2, x_lo: 2; x = x_hi * 2 + x_lo), y: 4, z: 16, core: 2. Of those that a mesh axis runs over, the one named last changes fastest.
Arguments:
- queries: bfloat16 [2048, 4096], P('seq', 'exp'), may hold values from -6 to 6
- key_states: bfloat16 [2048, 512], P('seq'), may hold values from -6 to 6
- value_states: bfloat16 [2048, 512], P('seq'), may hold values from -6 to 6
- residual: bfloat16 [2048, 4096], P('seq', 'exp'), may hold values from -54 to 54
- out_proj: bfloat16 [4096, 4096], P('exp'), may hold values from -0.5 to 0.5
- norm_gain: float32 [4096], replicated, may hold values from 0.1 to 1.9
- expert_ids: int32 [2048, 8], P('seq'), may hold values from 0 to 63, all different within a row; in each aligned block of 128 rows (0 to 127, 128 to 255, ...) at most 32 rows name the same one
- gate_scores: float32 [2048, 8], P('seq'), may hold values from 0.05 to 1
- w_gate: bfloat16 [64, 1024, 4096], P('exp', 'seq'), may hold values from -0.09375 to 0.09375
- w_up: bfloat16 [64, 1024, 4096], P('exp', 'seq'), may hold values from -0.09375 to 0.09375
- w_down: bfloat16 [64, 1024, 4096], P('exp', None, 'seq'), may hold values from -0.375 to 0.375
Outputs:
- attn_out: bfloat16 [2048, 4096], P('seq', 'exp')
- expert_out: bfloat16 [2048, 4096], P('seq', 'exp')
The draws below stay inside these ranges and needn't reach their ends.
Inputs may be any that keep to these rules, and one draw needn't show every extreme that they name: `expert_ids`: each row names 8 different experts. In each aligned block of 128 rows no expert is named by more than 32 rows, and in some block an expert is named by exactly 32 rows.
All inputs are finite; a program needn't handle non-finite values.
Results may differ from the reference program's by a relative error of at most 0.02.
Values may be sent and summed in bfloat16 or wider, within the bound.
A program may use at most 64 MiB of HBM per device.

```python
import math
import jax
import jax.numpy as jnp
import numpy as np
from jax import lax

D = 4096
HD = 128
KVH = 4
TOP = 8
FFW = 1024
ROWS = 128
HEADS = 32
EXPERTS = 64
LENGTH = 2048
CAP = 32
N_SEQ = 16


def draw_queries(key, part):
    key = jax.random.fold_in(key, 5)
    return jnp.clip(jax.random.normal(key, (LENGTH, HEADS * HD), jnp.float32), -6.0, 6.0).astype(jnp.bfloat16)


def draw_key_states(key, part):
    key = jax.random.fold_in(key, 6)
    return jnp.clip(jax.random.normal(key, (LENGTH, KVH * HD), jnp.float32), -6.0, 6.0).astype(jnp.bfloat16)


def draw_residual(key, part):
    key = jax.random.fold_in(key, 7)
    row_key, base_key = jax.random.split(key, 2)
    row_scale = jnp.exp(jax.random.uniform(row_key, (LENGTH, 1), jnp.float32, math.log(0.3), math.log(3.0)))
    col_pos = jnp.arange(D, dtype=jnp.float32)[None, :] / D
    base_draw = jnp.clip(jax.random.normal(base_key, (LENGTH, D), jnp.float32), -6.0, 6.0)
    col_scale = 0.3 * jnp.exp(col_pos * math.log(10.0))
    return (base_draw * row_scale * col_scale).astype(jnp.bfloat16)


def strengthened(values, key, source, target, shards_of, factor):
    def block_of(axis_at):
        return (jnp.arange(values.shape[axis_at]) // (values.shape[axis_at] // shards_of)).reshape((-1,) + (1,) * (values.ndim - 1 - axis_at))

    near = jax.random.permutation(key, shards_of)[block_of(target)]
    other_side = (block_of(target) + shards_of // 2) % shards_of
    return jnp.where((block_of(source) == near) | (block_of(source) == other_side), factor * values, values)


def steps_of(stream_key, dims, cuts, smallest, top_value):
    def one(axis_at, parts):
        draws = jax.random.uniform(jax.random.fold_in(jax.random.fold_in(stream_key, 6), axis_at), (parts,), jnp.float32, smallest / len(cuts), top_value / len(cuts))
        return jnp.repeat(jnp.exp(draws), dims[axis_at] // parts).reshape((-1,) + (1,) * (len(dims) - axis_at - 1))

    factor_of = one(*cuts[0])
    for cut in cuts[1:]:
        factor_of = factor_of * one(*cut)
    return factor_of


def deal_out(rng, own, number, rows, count, top, limit, slope):
    order = jax.random.permutation(rng, count)
    heavy_load, usual = shares(count, rows * top, limit, slope, True), shares(count, rows * top, limit, slope, False)
    places = jnp.arange(count)

    def named(sizes, rotation):
        used = int((sizes > 0).sum())
        fixed = max(1, used // 4)
        moved = fixed + (places - fixed + rotation * (used - fixed)) % max(1, count - fixed)
        return jnp.zeros((count,), jnp.int32).at[order[jnp.where(places < fixed, places, moved)]].set(jnp.asarray(sizes, jnp.int32))

    sizes = jnp.where(number % 4 == 0, named(heavy_load, number // 4), named(usual, number - number // 4 - 1))
    mixed = jax.random.permutation(jax.random.fold_in(own, 3), count)
    source_of, receiver = mixed[0:count // 2 * 2:2], mixed[1:count // 2 * 2:2]
    room = jnp.minimum(sizes[source_of] - 1, limit - sizes[receiver]) // 2
    room = jnp.where((source_of == order[0]) | (receiver == order[0]) | (sizes[receiver] == 0), 0, jnp.maximum(room, 0))
    moved = jax.random.randint(jax.random.fold_in(own, 4), (count // 2,), 0, 1 << 20) % (room + 1)
    sizes = sizes.at[source_of].add(-moved).at[receiver].add(moved)
    labels = jnp.searchsorted(jnp.cumsum(sizes), jnp.arange(rows * top), side="right").astype(jnp.int32)
    listing = labels.reshape(top, rows).T
    listing = listing[jax.random.permutation(jax.random.fold_in(own, 1), rows)]
    rotation = jax.random.randint(jax.random.fold_in(own, 2), (rows, 1), 0, top)
    return jnp.take_along_axis(listing, (jnp.arange(top)[None, :] + rotation) % top, axis=1)


def shares(amount, total, most, slope, full):
    loads = [(1 << 20) // math.isqrt(rank ** slope) + 1 for rank in range(1, amount + 1)]
    largest = most if full else min(most, max(-(-total // amount), total * loads[0] // sum(loads)))
    least = 1 if total - largest >= amount - 1 else 0
    given, surplus = [largest] + [least] * (amount - 1), total - largest - least * (amount - 1)
    while surplus > 0:
        movable = [i for i in range(1, amount) if given[i] < largest] or [i for i in range(1, amount) if given[i] < most]
        pool, budget = sum([loads[i] for i in movable]), surplus
        for i in movable:
            extra = min(most - given[i], max(1, budget * loads[i] // pool), surplus)
            given[i] = given[i] + extra
            surplus = surplus - extra
    return np.array(given)


def gaussian(key, extent, spread, most, cuts=(), kind=jnp.bfloat16):
    gain = steps_of(key, extent, cuts, -0.22, 0.18) if cuts else 1.0
    entries = jax.random.normal(key, extent, jnp.float32) * spread * gain
    return jnp.minimum(jnp.maximum(entries, -most), most).astype(kind)


def gaussian_with(rng, dims, deviation, most, shards, heavy, held_as=jnp.bfloat16):
    drawn = deviation * jax.random.normal(rng, dims, jnp.float32)
    if shards:
        drawn = drawn * steps_of(rng, dims, shards, -0.22, 0.18)
    return jnp.clip(strengthened(drawn, jax.random.fold_in(rng, 3), *heavy), -most, most).astype(held_as)


def setup_inputs(seed: int = 0) -> dict:
    keys = jax.random.split(jax.random.key(seed), 12)
    queries = draw_queries(jax.random.fold_in(keys[11], 71), 0)
    key_states = draw_key_states(jax.random.fold_in(keys[11], 71), 0)
    value_states = gaussian(keys[2], (LENGTH, KVH * HD), 1.0, 6.0, ((0, 16),))
    residual = draw_residual(jax.random.fold_in(keys[11], 71), 0)
    out_proj = gaussian(keys[4], (HEADS * HD, D), HD ** -0.5, 0.5, ((0, 32),))
    norm_gain = jnp.clip(1.0 + 0.18 * jax.random.normal(keys[5], (D,), jnp.float32), 0.1, 1.9)
    expert_ids_keys = jax.random.split(jax.random.fold_in(keys[6], 1), LENGTH // ROWS)
    expert_ids_turns = jax.random.permutation(jax.random.fold_in(keys[6], 3), LENGTH // ROWS)
    expert_ids = jax.vmap(lambda own, number: deal_out(jax.random.fold_in(keys[6], 2), own, number, ROWS, EXPERTS, TOP, CAP, 2))(expert_ids_keys, expert_ids_turns).reshape((LENGTH, TOP))
    gate_scores = jnp.clip(jnp.exp(math.log(1.0) - 2.9957323 * jax.random.uniform(keys[7], (LENGTH, TOP), jnp.float32) ** steps_of(keys[7], (LENGTH, TOP), ((0, 16),), -0.2, 0.2)), 0.05, 1.0)
    w_gate = gaussian(keys[8], (EXPERTS, FFW, D), D ** -0.5, 0.09375, ((0, 32), (1, 16)))
    w_up = gaussian(keys[9], (EXPERTS, FFW, D), D ** -0.5, 0.09375, ((0, 32), (1, 16)))
    w_down = gaussian_with(keys[10], (EXPERTS, FFW, D), FFW ** -0.5, 0.375, ((0, 32), (2, 16)), (0, 2, 32, 2.75))
    return dict(queries=queries, key_states=key_states, value_states=value_states, residual=residual, out_proj=out_proj, norm_gain=norm_gain, expert_ids=expert_ids, gate_scores=gate_scores, w_gate=w_gate, w_up=w_up, w_down=w_down)


NEG_FILL = -1e+30
NORM_EPS = 1e-06

def attend_head(query_rows, key_rows, value_rows):
    scores = jnp.dot(query_rows, key_rows.T, preferred_element_type=jnp.float32) * HD ** (-0.5)
    positions = jnp.arange(LENGTH)
    visible = positions[:, None] >= positions[None, :]
    scores = jnp.where(visible, scores, NEG_FILL)
    row_max = lax.optimization_barrier(jnp.max(scores, axis=1, keepdims=True))
    exp_weights = jnp.where(visible, jnp.exp(scores - row_max), 0.0)
    row_total = lax.optimization_barrier(jnp.sum(exp_weights, axis=1, keepdims=True))
    weighted = jnp.dot(exp_weights.astype(jnp.bfloat16), value_rows, preferred_element_type=jnp.float32)
    return (weighted / row_total).astype(jnp.bfloat16)

def reference(queries, key_states, value_states, residual, out_proj, norm_gain, expert_ids, gate_scores, w_gate, w_up, w_down):
    group_size = HEADS // KVH

    def one_head(head_index):
        query_rows = lax.dynamic_slice_in_dim(queries, (head_index * HD).astype(jnp.int32), HD, 1)
        kv_start = (head_index // group_size * HD).astype(jnp.int32)
        key_rows = lax.dynamic_slice_in_dim(key_states, kv_start, HD, 1)
        value_rows = lax.dynamic_slice_in_dim(value_states, kv_start, HD, 1)
        return attend_head(query_rows, key_rows, value_rows)
    head_outs = lax.map(one_head, jnp.arange(HEADS, dtype=jnp.int32))
    head_cat = jnp.transpose(head_outs, (1, 0, 2)).reshape(LENGTH, HEADS * HD)
    projected = jnp.dot(head_cat, out_proj, preferred_element_type=jnp.float32)
    residual_sum = residual.astype(jnp.float32) + projected
    mean_square = lax.optimization_barrier(jnp.mean(residual_sum * residual_sum, axis=1, keepdims=True))
    normed = (residual_sum * lax.rsqrt(mean_square + NORM_EPS) * norm_gain).astype(jnp.bfloat16)
    route_weight = gate_scores / lax.optimization_barrier(jnp.sum(gate_scores, axis=1, keepdims=True))
    flat_ids = expert_ids.reshape(-1).astype(jnp.int32)
    expert_axis = jnp.arange(EXPERTS, dtype=jnp.int32)
    matches = (flat_ids[:, None] == expert_axis[None, :]).astype(jnp.int32)
    route_rank = lax.optimization_barrier(jnp.sum((jnp.cumsum(matches, axis=0) - matches) * matches, axis=1)).astype(jnp.int32)
    buffer_rows = N_SEQ * CAP
    token_of = (jnp.arange(LENGTH * TOP, dtype=jnp.int32) // TOP).astype(jnp.int32)
    slot_table = jnp.zeros((EXPERTS, buffer_rows), jnp.int32).at[flat_ids, route_rank].set(token_of)
    weight_table = jnp.zeros((EXPERTS, buffer_rows), jnp.float32).at[flat_ids, route_rank].set(route_weight.reshape(-1))

    def add_expert(total_sum, expert_index):
        token_rows = jnp.take(normed, slot_table[expert_index], axis=0)
        gate_value = jnp.dot(token_rows, w_gate[expert_index].T, preferred_element_type=jnp.float32)
        up_value = jnp.dot(token_rows, w_up[expert_index].T, preferred_element_type=jnp.float32)
        hidden = (jax.nn.silu(gate_value) * up_value).astype(jnp.bfloat16)
        produced = jnp.dot(hidden, w_down[expert_index], preferred_element_type=jnp.float32).astype(jnp.bfloat16)
        weighted = weight_table[expert_index][:, None] * produced.astype(jnp.float32)
        return (total_sum.at[slot_table[expert_index]].add(weighted), None)
    expert_sum, unused = lax.scan(add_expert, jnp.zeros((LENGTH, D), jnp.float32), expert_axis)
    return (projected.astype(jnp.bfloat16), expert_sum.astype(jnp.bfloat16))
```

```python
import jax
import jax.numpy as jnp
from jax import lax
from jax.experimental import pallas as pl
from jax.experimental.pallas import tpu as pltpu
from jax.sharding import PartitionSpec as P

MESH = pl.DeviceIdType.MESH
BF16 = jnp.bfloat16
F32 = jnp.float32
NEG_FILL = -1e30
NORM_EPS = 1e-06
D = 4096
HD = 128
ROWS = 128
NZ = 16
STEPS = 8
CAP = 32
CHUNKS = 4


def dot(a, b):
    return jnp.dot(a, b, preferred_element_type=F32)


def dot_t(a, b):
    return lax.dot_general(a, b, (((1,), (1,)), ((), ())), preferred_element_type=F32)


def remote(src, dst, send_sem, recv_sem, device):
    return pltpu.make_async_remote_copy(
        src_ref=src,
        dst_ref=dst,
        send_sem=send_sem,
        recv_sem=recv_sem,
        device_id=device,
        device_id_type=MESH,
    )


class Place:
    def __init__(self):
        self.s = lax.axis_index("seq")
        self.e = lax.axis_index("exp")
        self.yh = lax.div(self.s, 2)
        self.c = lax.rem(self.s, 2)
        self.y = lax.div(self.s, 4)
        self.h = lax.rem(self.yh, 2)
        self.z = lax.div(self.e, 2)
        self.l = lax.rem(self.e, 2)

    def seq_of(self, y, h, c):
        return (y * 2 + h) * 2 + c

    def y_step(self, k):
        return lax.rem(self.y + k + 4, 4)

    def z_step(self, k):
        return lax.rem(self.z + k + 32, NZ)

    def at_y(self, k):
        return (self.seq_of(self.y_step(k), self.h, self.c), self.e)

    def at_other_h(self):
        return (self.seq_of(self.y, 1 - self.h, self.c), self.e)

    def at_other_core(self):
        return (self.seq_of(self.y, self.h, 1 - self.c), self.e)

    def at_z(self, k):
        return (self.s, self.z_step(k) * 2 + self.l)

    def at_other_l(self):
        return (self.s, self.z * 2 + 1 - self.l)


class SeqGather:
    def __init__(self, me, buf, send, recv):
        self.me, self.buf, self.send, self.recv = me, buf, send, recv

    def part(self, j, y, h):
        return self.buf.at[j, y * 2 + h, self.me.c]

    def copy(self, j, k, ref, device):
        return remote(ref, ref, self.send.at[j, k], self.recv.at[j, k], device)

    def push(self, j, k):
        me = self.me
        if k < 3:
            ref = self.part(j, me.y, me.h)
        elif k < 5:
            ref = self.part(j, me.y, 1 - me.h)
        elif k == 5:
            ref = self.part(j, me.y_step(-1), me.h)
        elif k == 6:
            ref = self.part(j, me.y_step(1), 1 - me.h)
        else:
            ref = self.buf.at[j, :, me.c]
        if k == 0:
            device = me.at_other_h()
        elif k in (1, 3, 5):
            device = me.at_y(1)
        elif k in (2, 4, 6):
            device = me.at_y(-1)
        else:
            device = me.at_other_core()
        return self.copy(j, k, ref, device)

    def arrived(self, j, k):
        me = self.me
        ref = [
            lambda: self.part(j, me.y, 1 - me.h),
            lambda: self.part(j, me.y_step(-1), me.h),
            lambda: self.part(j, me.y_step(1), me.h),
            lambda: self.part(j, me.y_step(-1), 1 - me.h),
            lambda: self.part(j, me.y_step(1), 1 - me.h),
            lambda: self.part(j, me.y_step(2), me.h),
            lambda: self.part(j, me.y_step(2), 1 - me.h),
            lambda: self.buf.at[j, :, 1 - me.c],
        ][k]()
        self.copy(j, k, ref, me.at_other_core()).wait_recv()

    def a(self, j):
        for k in range(3):
            self.push(j, k).start()

    def b(self, j):
        self.arrived(j, 0)
        self.push(j, 3).start()
        self.push(j, 4).start()

    def c(self, j):
        self.arrived(j, 1)
        self.push(j, 5).start()
        self.arrived(j, 4)
        self.push(j, 6).start()
        self.arrived(j, 2)
        self.arrived(j, 3)

    def d(self, j):
        self.arrived(j, 5)
        self.arrived(j, 6)
        self.push(j, 7).start()

    def e(self, j):
        self.arrived(j, 7)

    def finish(self, j):
        for k in range(8):
            self.push(j, k).wait_send()


class ZRing:
    def __init__(self, me, buf, send, recv):
        self.me, self.buf, self.send, self.recv = me, buf, send, recv

    def up(self, k):
        ref = self.buf.at[self.me.z_step(1 - k)]
        return remote(ref, ref, self.send.at[0, k], self.recv.at[0, k], self.me.at_z(1))

    def down(self, k):
        ref = self.buf.at[self.me.z_step(k - 1)]
        return remote(ref, ref, self.send.at[1, k], self.recv.at[1, k], self.me.at_z(-1))

    def start(self):
        self.down(1).start()
        self.up(1).start()

    def step(self, j):
        me = self.me
        low, high = me.z_step(-j), me.z_step(j + 1)

        @pl.when(j >= 1)
        def _():
            ref = self.buf.at[low]
            remote(ref, ref, self.send.at[0, j], self.recv.at[0, j], me.at_z(1)).wait_recv()

            @pl.when(j < STEPS - 1)
            def _():
                self.up(j + 1).start()

        ref = self.buf.at[high]
        remote(ref, ref, self.send.at[1, j + 1], self.recv.at[1, j + 1], me.at_z(-1)).wait_recv()

        @pl.when(j < STEPS - 1)
        def _():
            self.down(j + 2).start()

        return low, high

    def finish(self):
        def one(k, _):
            self.down(k).wait_send()

            @pl.when(k < STEPS)
            def _():
                self.up(k).wait_send()

            return 0

        lax.fori_loop(1, STEPS + 1, one, 0)


def kernel(
    q_ref, res_ref, gain_ref, ids_ref, score_ref,
    key_hbm, val_hbm, proj_hbm, wg_hbm, wu_hbm, wd_hbm,
    attn_ref, out_ref,
    kv, strip, wp, heads, partial, partial_in, xcols, xs, sx,
    wg, wu, wd, wcat, wdz, acc, ssq, hid, prod, ret, table, spread,
    ring_in, ring_out,
    local_sem, kv_send, kv_recv, wz_send, wz_recv, wp_send, wp_recv,
    hz_send, hz_recv, pl_send, pl_recv, xz_send, xz_recv, xl_send, xl_recv,
    xs_send, xs_recv, hid_send, hid_recv, ret_send, ret_recv, rz_send, rz_recv,
):
    me = Place()
    s, z, l = me.s, me.z, me.l

    group = pl.multiple_of(lax.div(z, 4) * HD, HD)
    loads = [
        pltpu.make_async_copy(key_hbm.at[:, pl.ds(group, HD)], kv.at[0, me.yh, me.c, 0], local_sem.at[0]),
        pltpu.make_async_copy(val_hbm.at[:, pl.ds(group, HD)], kv.at[0, me.yh, me.c, 1], local_sem.at[1]),
        pltpu.make_async_copy(
            proj_hbm.at[pl.ds(pl.multiple_of(me.yh * 16, 16), 16), :], strip, local_sem.at[2]
        ),
        pltpu.make_async_copy(wg_hbm, wg, local_sem.at[3]),
        pltpu.make_async_copy(wu_hbm, wu, local_sem.at[4]),
        pltpu.make_async_copy(wd_hbm, wd, local_sem.at[5]),
    ]
    for cp in loads:
        cp.start()

    def z_peer(d):
        return (s, me.z_step(d) * 2 + l)

    def cross_peer(d):
        return (lax.rem(s + lax.div(d, 2), 16), z * 2 + lax.rem(l + d, 2))

    def seq_peer_back(d):
        return (lax.rem(s + 16 - lax.div(d, 2), 16), z * 2 + lax.rem(l + d, 2))

    barrier = pltpu.get_barrier_semaphore()

    def greet_z(d, _):
        pl.semaphore_signal(barrier, inc=1, device_id=z_peer(d), device_id_type=MESH)
        return 0

    def greet_cross(d, _):
        pl.semaphore_signal(barrier, inc=1, device_id=cross_peer(d), device_id_type=MESH)
        return 0

    lax.fori_loop(1, 32, greet_cross, 0)
    lax.fori_loop(1, NZ, greet_z, 0)
    pl.semaphore_wait(barrier, 31 + NZ - 1)

    kv_gather = SeqGather(me, kv, kv_send, kv_recv)
    wp_gather = SeqGather(me, wp, wp_send, wp_recv)
    loads[0].wait()
    loads[1].wait()
    kv_gather.a(0)
    loads[2].wait()

    def strip_copy(d):
        target = me.z_step(d)
        col = pl.multiple_of(target * 256 + me.c * HD, HD)
        return remote(
            strip.at[:, pl.ds(col, HD)],
            wp.at[0, me.yh, me.c, z],
            wz_send.at[d],
            wz_recv.at[d],
            z_peer(d),
        )

    def strip_start(d, _):
        strip_copy(d).start()
        return 0

    lax.fori_loop(1, NZ, strip_start, 0)
    wp[0, me.yh, me.c, z] = strip[:, pl.ds(pl.multiple_of(z * 256 + me.c * HD, HD), HD)]

    lane = lax.broadcasted_iota(jnp.int32, (ROWS, 128), 1)
    row = lax.broadcasted_iota(jnp.int32, (ROWS, 128), 0)
    ids = ids_ref[...]
    weight = score_ref[...] / jnp.sum(score_ref[...], axis=1, keepdims=True)
    routed = jnp.zeros((ROWS, 128), F32)
    shares = jnp.zeros((ROWS, 128), F32)
    for q in range(4):
        pair = l if q < 2 else 1 - l
        expert = 4 * z + 2 * pair + q % 2
        match = ids == expert
        lanes = lax.div(lane, CAP) == q
        routed = jnp.where(lanes, jnp.sum(jnp.where(match, 1.0, 0.0), axis=1, keepdims=True), routed)
        shares = jnp.where(lanes, jnp.sum(jnp.where(match, weight, 0.0), axis=1, keepdims=True), shares)
    earlier = jnp.where(lane < row, 1.0, 0.0).astype(BF16)
    rank = dot(earlier, routed.astype(BF16))
    chosen = (routed > 0.5) & (rank == lax.rem(lane, CAP).astype(F32))
    table[...] = jnp.where(chosen, 1.0, 0.0).T.astype(BF16)
    spread_all = jnp.where(chosen, shares, 0.0)
    spread_high = spread_all.astype(BF16)
    spread[0] = spread_high
    spread[1] = (spread_all - spread_high.astype(F32)).astype(BF16)

    kv_gather.b(0)

    def strip_wait(d, _):
        ref = wp.at[0, me.yh, me.c, me.z_step(-d)]
        remote(ref, ref, wz_send.at[d], wz_recv.at[d], z_peer(d)).wait_recv()
        return 0

    kv_gather.c(0)
    lax.fori_loop(1, NZ, strip_wait, 0)
    wp_gather.a(0)
    kv_gather.d(0)

    loads[3].wait()
    loads[4].wait()
    gain = gain_ref[...]
    zeros = jnp.zeros((64, D), BF16)
    for i in range(2):
        wcat[i, pl.ds(64 * i, 64), :] = (wg[i].astype(F32) * gain).astype(BF16)
        wcat[i, pl.ds(64 * (1 - i), 64), :] = zeros
        wcat[i, pl.ds(128 + 64 * i, 64), :] = (wu[i].astype(F32) * gain).astype(BF16)
        wcat[i, pl.ds(128 + 64 * (1 - i), 64), :] = zeros
    loads[5].wait()

    def lay_down(t, _):
        at = pl.multiple_of(t * 64, 64)
        none = jnp.zeros((64, 256), BF16)
        wdz[t, 0:64, 0:256] = wd[0, pl.ds(at, 64), :]
        wdz[t, 0:64, 256:512] = none
        wdz[t, 64:128, 0:256] = none
        wdz[t, 64:128, 256:512] = wd[1, pl.ds(at, 64), :]
        return 0

    lax.fori_loop(0, 16, lay_down, 0)
    acc[...] = jnp.zeros_like(acc)
    ssq[...] = jnp.zeros_like(ssq)
    partial[...] = jnp.zeros_like(partial)

    wp_gather.b(0)
    kv_gather.e(0)

    keys = kv[0, :, :, 0].reshape(16 * ROWS, HD)
    scores = dot_t(q_ref[...], keys) * HD ** (-0.5)
    key_pos = lax.broadcasted_iota(jnp.int32, (ROWS, 16 * ROWS), 1)
    query_pos = lax.broadcasted_iota(jnp.int32, (ROWS, 16 * ROWS), 0) + s * ROWS
    scores = jnp.where(query_pos >= key_pos, scores, NEG_FILL)
    row_max = jnp.max(scores, axis=1, keepdims=True)
    exp_weights = jnp.exp(scores - row_max)
    row_total = jnp.sum(exp_weights, axis=1, keepdims=True)
    values = kv[0, :, :, 1].reshape(16 * ROWS, HD)
    heads[z] = (dot(exp_weights.astype(BF16), values) / row_total).astype(BF16)

    head_ring = ZRing(me, heads, hz_send, hz_recv)
    head_ring.start()
    wp_gather.c(0)
    wp_gather.d(0)
    wp_gather.e(0)

    def project(j, _):
        low, high = head_ring.step(j)
        for block in (low, high):
            for half in range(2):
                columns = wp[0, :, half, block].reshape(HD, HD)
                partial[half] += dot(heads[block], columns)
        return 0

    lax.fori_loop(0, STEPS, project, 0)
    swap = remote(partial.at[1 - l], partial_in, pl_send, pl_recv, me.at_other_l())
    swap.start()
    swap.wait_recv()
    projected = partial[l] + partial_in[...]
    attn_ref[...] = projected.astype(BF16)
    xcols[z] = (projected + res_ref[...].astype(F32)).astype(BF16)

    x_ring = ZRing(me, xcols, xz_send, xz_recv)
    x_ring.start()
    xs_gather = SeqGather(me, xs, xs_send, xs_recv)

    def x_swap(j):
        return remote(
            sx.at[j],
            xs.at[j, me.yh, me.c, :, :, pl.ds(pl.multiple_of(l * HD, HD), HD)],
            xl_send.at[j],
            xl_recv.at[j],
            me.at_other_l(),
        )

    def dispatch(t, _):
        @pl.when(t < STEPS)
        def _():
            low, high = x_ring.step(t)
            for ab, block in enumerate((low, high)):
                picked = dot(table[...], xcols[block]).astype(BF16)
                xs[t, me.yh, me.c, ab, :, pl.ds(pl.multiple_of(l * HD, HD), HD)] = picked[:64]
                sx[t, ab] = picked[64:]
            x_swap(t).start()

        @pl.when((t >= 1) & (t < STEPS + 1))
        def _():
            j = t - 1
            ref = xs.at[j, me.yh, me.c, :, :, pl.ds(pl.multiple_of((1 - l) * HD, HD), HD)]
            remote(ref, ref, xl_send.at[j], xl_recv.at[j], me.at_other_l()).wait_recv()
            xs_gather.a(j)

        @pl.when((t >= 2) & (t < STEPS + 2))
        def _():
            xs_gather.b(t - 2)

        @pl.when((t >= 3) & (t < STEPS + 3))
        def _():
            xs_gather.c(t - 3)

        @pl.when((t >= 4) & (t < STEPS + 4))
        def _():
            xs_gather.d(t - 4)

        @pl.when(t >= 5)
        def _():
            j = t - 5
            xs_gather.e(j)
            for ab, block in enumerate((me.z_step(-j), me.z_step(j + 1))):
                col = pl.multiple_of(block * 256, 256)
                for i in range(2):
                    x = xs[j, :, :, ab, pl.ds(i * CAP, CAP), :].reshape(16 * CAP, 256)
                    acc[...] += dot_t(x, wcat[i, :, pl.ds(col, 256)])
                    wide = x.astype(F32)
                    square = wide * wide
                    ssq[i] += square[:, :128] + square[:, 128:]

        return 0

    lax.fori_loop(0, STEPS + 5, dispatch, 0)

    half = lax.broadcasted_iota(jnp.int32, (ROWS, 128), 1) < 64
    hid_gather = SeqGather(me, hid, hid_send, hid_recv)
    for k in range(CHUNKS):
        rows = pl.ds(k * ROWS, ROWS)
        scales = [
            lax.rsqrt(jnp.sum(ssq[i, rows, :], axis=1, keepdims=True) * (1.0 / D) + NORM_EPS)
            for i in range(2)
        ]
        scale = jnp.where(half, scales[0], scales[1])
        gate = acc[rows, 0:128] * scale
        up = acc[rows, 128:256] * scale
        hid[k, me.yh, me.c] = (gate / (1.0 + jnp.exp(-gate)) * up).astype(BF16)
        hid_gather.a(k)

    def hidden(t, _):
        @pl.when(t < CHUNKS)
        def _():
            hid_gather.b(t)

        @pl.when((t >= 1) & (t < CHUNKS + 1))
        def _():
            hid_gather.c(t - 1)

        @pl.when((t >= 2) & (t < CHUNKS + 2))
        def _():
            hid_gather.d(t - 2)

        @pl.when(t >= 3)
        def _():
            k = t - 3
            hid_gather.e(k)
            total = jnp.zeros((ROWS, 512), F32)
            for yh in range(8):
                for c in range(2):
                    total += dot(hid[k, yh, c], wdz[yh * 2 + c])
            made = total.astype(BF16)
            for i in range(2):
                prod[pl.ds(k * 4, 4), pl.ds(i * CAP, CAP), :] = made[:, i * 256:(i + 1) * 256].reshape(4, CAP, 256)

        return 0

    lax.fori_loop(0, CHUNKS + 3, hidden, 0)

    def back_copy(d):
        target_s = lax.rem(s + lax.div(d, 2), 16)
        target_l = lax.rem(l + d, 2)
        return remote(
            prod.at[target_s, :, pl.ds(pl.multiple_of(target_l * HD, HD), HD)],
            ret.at[s, pl.ds(pl.multiple_of(lax.rem(d, 2) * 64, 64), 64), :],
            ret_send.at[d],
            ret_recv.at[s, lax.rem(d, 2)],
            cross_peer(d),
        )

    def back_start(d, _):
        back_copy(d).start()
        return 0

    lax.fori_loop(1, 32, back_start, 0)
    ret[s, 0:64, :] = prod[s, :, pl.ds(pl.multiple_of(l * HD, HD), HD)]

    def back_wait(source, half):
        ref = ret.at[source, pl.ds(half * 64, 64), :]
        remote(ref, ref, ret_send.at[1], ret_recv.at[source, half], me.at_other_l()).wait_recv()

    def share_of(target):
        @pl.when(target != s)
        def _():
            back_wait(target, 0)

        back_wait(target, 1)
        returned = ret[target]
        return dot(spread[0], returned) + dot(spread[1], returned)

    def sum_up(k):
        return remote(ring_out.at[0, k], ring_in.at[0, k], rz_send.at[0, k], rz_recv.at[0, k], me.at_z(1))

    def sum_down(k):
        return remote(ring_out.at[1, k], ring_in.at[1, k], rz_send.at[1, k], rz_recv.at[1, k], me.at_z(-1))

    def reduce_up(k, _):
        share = share_of(me.z_step(8 - k))

        @pl.when(k == 0)
        def _():
            ring_out[0, 1] = share.astype(BF16)

        @pl.when(k >= 1)
        def _():
            sum_up(k).wait_recv()
            ring_out[0, k + 1] = (share + ring_in[0, k].astype(F32)).astype(BF16)

        sum_up(k + 1).start()

        @pl.when(k < 7)
        def _():
            other = share_of(me.z_step(-7 + k))

            @pl.when(k == 0)
            def _():
                ring_out[1, 1] = other.astype(BF16)

            @pl.when(k >= 1)
            def _():
                sum_down(k).wait_recv()
                ring_out[1, k + 1] = (other + ring_in[1, k].astype(F32)).astype(BF16)

            sum_down(k + 1).start()

        return 0

    lax.fori_loop(0, 8, reduce_up, 0)
    total = share_of(z)
    sum_down(7).wait_recv()
    total += ring_in[1, 7].astype(F32)
    sum_up(8).wait_recv()
    total += ring_in[0, 8].astype(F32)
    out_ref[...] = total.astype(BF16)

    kv_gather.finish(0)
    wp_gather.finish(0)
    head_ring.finish()
    x_ring.finish()
    swap.wait_send()

    def strip_sent(d, _):
        strip_copy(d).wait_send()
        return 0

    def back_sent(d, _):
        back_copy(d).wait_send()
        return 0

    def xs_sent(j, _):
        x_swap(j).wait_send()
        xs_gather.finish(j)
        return 0

    def hid_sent(j, _):
        hid_gather.finish(j)
        return 0

    def sums_sent(k, _):
        sum_up(k).wait_send()

        @pl.when(k < 8)
        def _():
            sum_down(k).wait_send()

        return 0

    lax.fori_loop(1, NZ, strip_sent, 0)
    lax.fori_loop(1, 32, back_sent, 0)
    lax.fori_loop(0, STEPS, xs_sent, 0)
    lax.fori_loop(0, CHUNKS, hid_sent, 0)
    lax.fori_loop(1, 9, sums_sent, 0)


def per_device(
    queries, key_states, value_states, residual, out_proj, norm_gain,
    expert_ids, gate_scores, w_gate, w_up, w_down,
):
    vmem = pl.BlockSpec(memory_space=pltpu.VMEM)
    anywhere = pl.BlockSpec(memory_space=pl.ANY)
    dma = pltpu.SemaphoreType.DMA
    block = jax.ShapeDtypeStruct((ROWS, HD), BF16)
    scratch = [
        pltpu.VMEM((1, 8, 2, 2, ROWS, HD), BF16),
        pltpu.VMEM((16, D), BF16),
        pltpu.VMEM((1, 8, 2, NZ, 16, HD), BF16),
        pltpu.VMEM((NZ, ROWS, HD), BF16),
        pltpu.VMEM((2, ROWS, HD), F32),
        pltpu.VMEM((ROWS, HD), F32),
        pltpu.VMEM((NZ, ROWS, HD), BF16),
        pltpu.VMEM((STEPS, 8, 2, 2, 64, 256), BF16),
        pltpu.VMEM((STEPS, 2, 64, HD), BF16),
        pltpu.VMEM((2, 64, D), BF16),
        pltpu.VMEM((2, 64, D), BF16),
        pltpu.VMEM((2, 1024, 256), BF16),
        pltpu.VMEM((2, 256, D), BF16),
        pltpu.VMEM((16, 128, 512), BF16),
        pltpu.VMEM((512, 256), F32),
        pltpu.VMEM((2, 512, 128), F32),
        pltpu.VMEM((CHUNKS, 8, 2, ROWS, 128), BF16),
        pltpu.VMEM((16, 64, 256), BF16),
        pltpu.VMEM((NZ, 128, HD), BF16),
        pltpu.VMEM((128, ROWS), BF16),
        pltpu.VMEM((2, ROWS, 128), BF16),
        pltpu.VMEM((2, 9, ROWS, HD), BF16),
        pltpu.VMEM((2, 9, ROWS, HD), BF16),
        dma((6,)),
        dma((1, 8)), dma((1, 8)),
        dma((NZ,)), dma((NZ,)),
        dma((1, 8)), dma((1, 8)),
        dma((2, 9)), dma((2, 9)),
        dma, dma,
        dma((2, 9)), dma((2, 9)),
        dma((STEPS,)), dma((STEPS,)),
        dma((STEPS, 8)), dma((STEPS, 8)),
        dma((CHUNKS, 8)), dma((CHUNKS, 8)),
        dma((32,)), dma((16, 2)),
        dma((2, 9)), dma((2, 9)),
    ]
    return pl.pallas_call(
        kernel,
        out_shape=(block, block),
        in_specs=[vmem] * 5 + [anywhere] * 6,
        out_specs=(vmem, vmem),
        scratch_shapes=scratch,
        compiler_params=pltpu.CompilerParams(
            collective_id=0, has_side_effects=True, vmem_limit_bytes=48 * 2**20
        ),
        cost_estimate=pl.CostEstimate(flops=2 * 10**9, bytes_accessed=8 * 10**6, transcendentals=10**6),
        name="layer",
    )(
        queries, residual, norm_gain.reshape(1, D), expert_ids, gate_scores,
        key_states, value_states, out_proj, w_gate, w_up, w_down,
    )


def solution(mesh):
    placed = (
        P("seq", "exp"),
        P("seq", None),
        P("seq", None),
        P("seq", "exp"),
        P("exp", None),
        P(),
        P("seq", None),
        P("seq", None),
        P("exp", "seq", None),
        P("exp", "seq", None),
        P("exp", None, "seq"),
    )
    return jax.shard_map(
        per_device,
        mesh=mesh,
        in_specs=placed,
        out_specs=(P("seq", "exp"), P("seq", "exp")),
        check_vma=False,
    )
```

```python
import jax
import jax.numpy as jnp
from jax import lax
from jax.experimental import pallas as pl
from jax.experimental.pallas import tpu as pltpu
from jax.sharding import PartitionSpec as P

MESH = pl.DeviceIdType.MESH
BF16 = jnp.bfloat16
F32 = jnp.float32
NEG_FILL = -1e30
NORM_EPS = 1e-06
D = 4096
HD = 128
ROWS = 128
NZ = 16
STEPS = 8
CAP = 32
CHUNKS = 4
HALF = 64


def dot(a, b):
    return jnp.dot(a, b, preferred_element_type=F32)


def dot_t(a, b):
    return lax.dot_general(a, b, (((1,), (1,)), ((), ())), preferred_element_type=F32)


def remote(src, dst, send_sem, recv_sem, device):
    return pltpu.make_async_remote_copy(
        src_ref=src,
        dst_ref=dst,
        send_sem=send_sem,
        recv_sem=recv_sem,
        device_id=device,
        device_id_type=MESH,
    )


class Place:
    def __init__(self):
        self.s = lax.axis_index("seq")
        self.e = lax.axis_index("exp")
        self.yh = lax.div(self.s, 2)
        self.c = lax.rem(self.s, 2)
        self.y = lax.div(self.s, 4)
        self.h = lax.rem(self.yh, 2)
        self.z = lax.div(self.e, 2)
        self.l = lax.rem(self.e, 2)

    def seq_of(self, y, h, c):
        return (y * 2 + h) * 2 + c

    def y_step(self, k):
        return lax.rem(self.y + k + 4, 4)

    def z_step(self, k):
        return lax.rem(self.z + k + 32, NZ)

    def at_seq(self, yh, c):
        return (yh * 2 + c, self.e)

    def at_y(self, k):
        return (self.seq_of(self.y_step(k), self.h, self.c), self.e)

    def at_other_h(self):
        return (self.seq_of(self.y, 1 - self.h, self.c), self.e)

    def at_other_core(self):
        return (self.seq_of(self.y, self.h, 1 - self.c), self.e)

    def at_z(self, k):
        return (self.s, self.z_step(k) * 2 + self.l)

    def at_other_l(self):
        return (self.s, self.z * 2 + 1 - self.l)


class GroupGather:
    def __init__(self, me, buf, send, recv):
        self.me, self.buf, self.send, self.recv = me, buf, send, recv

    def copy(self, j, k, ref, device):
        return remote(ref, ref, self.send.at[j, k], self.recv.at[j, k], device)

    def push(self, j, k):
        me = self.me
        if k < 2:
            return self.copy(j, k, self.buf.at[j, me.y, me.c], me.at_y(1 - 2 * k))
        if k < 4:
            way = 5 - 2 * k
            return self.copy(j, k, self.buf.at[j, me.y_step(-way), me.c, k - 2], me.at_y(way))
        return self.copy(j, k, self.buf.at[j, :, me.c], me.at_other_core())

    def arrived(self, j, k):
        me = self.me
        if k < 2:
            ref = self.buf.at[j, me.y_step(2 * k - 1), me.c]
        elif k < 4:
            ref = self.buf.at[j, me.y_step(2), me.c, k - 2]
        else:
            ref = self.buf.at[j, :, 1 - me.c]
        self.copy(j, k, ref, me.at_other_core()).wait_recv()

    def a(self, j):
        self.push(j, 0).start()
        self.push(j, 1).start()

    def c(self, j):
        for k in range(2):
            self.arrived(j, k)
            self.push(j, 2 + k).start()

    def d(self, j):
        self.arrived(j, 2)
        self.arrived(j, 3)
        self.push(j, 4).start()

    def e(self, j):
        self.arrived(j, 4)

    def finish(self, j):
        for k in range(5):
            self.push(j, k).wait_send()


class ZRing:
    def __init__(self, me, buf, send, recv):
        self.me, self.buf, self.send, self.recv = me, buf, send, recv

    def piece(self, way, k, half, block):
        ref = self.buf.at[block, pl.ds(half * HALF, HALF), :]
        return remote(
            ref, ref, self.send.at[way, k, half], self.recv.at[way, k, half], self.me.at_z(1 - 2 * way)
        )

    def up(self, k, half):
        return self.piece(0, k, half, self.me.z_step(1 - k))

    def down(self, k, half):
        return self.piece(1, k, half, self.me.z_step(k - 1))

    def start(self, half):
        self.down(1, half).start()
        self.up(1, half).start()

    def step(self, j):
        low, high = self.me.z_step(-j), self.me.z_step(j + 1)
        for half in range(2):

            @pl.when(j >= 1)
            def _():
                self.piece(0, j, half, low).wait_recv()

                @pl.when(j < STEPS - 1)
                def _():
                    self.up(j + 1, half).start()

            self.piece(1, j + 1, half, high).wait_recv()

            @pl.when(j < STEPS - 1)
            def _():
                self.down(j + 2, half).start()

        return low, high

    def finish(self):
        def one(k, _):
            for half in range(2):
                self.down(k, half).wait_send()

                @pl.when(k < STEPS)
                def _():
                    self.up(k, half).wait_send()

            return 0

        lax.fori_loop(1, STEPS + 1, one, 0)


class ZSum:
    def __init__(self, me, share, inbox, outbox, send, recv):
        self.me, self.share = me, share
        self.inbox, self.outbox, self.send, self.recv = inbox, outbox, send, recv

    def copy(self, way, k, half):
        return remote(
            self.outbox.at[way, k, half],
            self.inbox.at[way, k, half],
            self.send.at[way, k, half],
            self.recv.at[way, k, half],
            self.me.at_z(1 - 2 * way),
        )

    def step(self, k, beside, first=False, last=False):
        shares = [self.share(self.me.z_step(8 - k))]
        if not last:
            shares.append(self.share(self.me.z_step(k - 7)))
        for half in range(2):
            for way, share in enumerate(shares):
                part = share[half * HALF:(half + 1) * HALF]
                if not first:
                    self.copy(way, k, half).wait_recv()
                    part = part + self.inbox[way, k, half].astype(F32)
                self.outbox[way, k + 1, half] = part.astype(BF16)
                self.copy(way, k + 1, half).start()
        beside(k)

    def run(self, beside=lambda k: None):
        self.step(0, beside, first=True)

        def one(k, _):
            self.step(k, beside)
            return 0

        lax.fori_loop(1, 7, one, 0)
        self.step(7, beside, last=True)
        own = self.share(self.me.z)
        parts = []
        for half in range(2):
            self.copy(1, 7, half).wait_recv()
            self.copy(0, 8, half).wait_recv()
            part = own[half * HALF:(half + 1) * HALF]
            parts.append(part + self.inbox[1, 7, half].astype(F32) + self.inbox[0, 8, half].astype(F32))
        return parts

    def finish(self):
        def one(k, _):
            for half in range(2):
                self.copy(0, k, half).wait_send()

                @pl.when(k < 8)
                def _():
                    self.copy(1, k, half).wait_send()

            return 0

        lax.fori_loop(1, 9, one, 0)


def kernel(
    q_hbm, res_hbm, gain_hbm, ids_hbm, score_hbm,
    key_hbm, val_hbm, proj_hbm, wg_hbm, wu_hbm, wd_hbm,
    attn_ref, out_ref,
    q_ref, res_ref, gain_ref, ids_ref, score_ref,
    kv, proj, head, partial, partial_in, xcols, xs, sx,
    wg, wu, wcat, wdown, acc, ssq, hid, prod, ret, table, spread,
    sum_in, sum_out, ring_in, ring_out,
    local_sem, kv_send, kv_recv, core_send, core_recv, wx_send, wx_recv, wy_send, wy_recv,
    ps_send, ps_recv, pl_send, pl_recv, xz_send, xz_recv, xl_send, xl_recv,
    xs_send, xs_recv, hid_send, hid_recv, ret_send, ret_recv, rz_send, rz_recv,
):
    me = Place()
    s, z, l = me.s, me.z, me.l
    block = me.y * 2 + me.c

    group = pl.multiple_of(lax.div(z, 4) * HD, HD)
    loads = [
        pltpu.make_async_copy(src, dst, local_sem.at[k])
        for k, (src, dst) in enumerate(
            [
                (key_hbm.at[:, pl.ds(group, HD)], kv.at[me.yh, me.c, 0]),
                (val_hbm.at[:, pl.ds(group, HD)], kv.at[me.yh, me.c, 1]),
                (gain_hbm, gain_ref),
                (wg_hbm, wg),
                (wu_hbm, wu),
                (q_hbm, q_ref),
                (proj_hbm, proj),
                (res_hbm, res_ref),
                (ids_hbm, ids_ref),
                (score_hbm, score_ref),
            ]
        )
    ]
    for h in range(2):
        for c in range(2):
            dst = wdown.at[:, :, c, lax.rem(me.h + h, 2), :, pl.ds(0, 256)]
            loads.append(pltpu.make_async_copy(wd_hbm.at[:, :, h, c], dst, local_sem.at[10 + 2 * h + c]))
    for cp in loads:
        cp.start()

    def seq_peer(d):
        return (lax.rem(s + d, 16), me.e)

    def group_peer(d):
        other = lax.rem(block + lax.div(d, 2), 8)
        place = me.seq_of(lax.div(other, 2), me.h, lax.rem(other, 2))
        return (place, z * 2 + lax.rem(l + d, 2))

    barrier = pltpu.get_barrier_semaphore()

    def greet_seq(d, _):
        pl.semaphore_signal(barrier, inc=1, device_id=seq_peer(d), device_id_type=MESH)
        return 0

    def greet_group(d, _):
        pl.semaphore_signal(barrier, inc=1, device_id=group_peer(2 * d + 1), device_id_type=MESH)
        return 0

    lax.fori_loop(1, 16, greet_seq, 0)
    lax.fori_loop(0, 8, greet_group, 0)
    for k in (1, -1):
        pl.semaphore_signal(barrier, inc=1, device_id=me.at_z(k), device_id_type=MESH)

    loads[2].wait()
    loads[3].wait()
    loads[4].wait()
    gain = gain_ref[...]
    for i in range(2):
        wcat[i, 0, 0:64, :] = (wg[i].astype(F32) * gain).astype(BF16)
        wcat[i, 0, 64:128, :] = (wu[i].astype(F32) * gain).astype(BF16)

    loads[0].wait()
    loads[1].wait()
    pl.semaphore_wait(barrier, 15 + 8 + 2)

    def kv_copy(d):
        ref = kv.at[me.yh, me.c]
        target = lax.rem(me.yh + d, 8)
        return remote(ref, ref, kv_send.at[d], kv_recv.at[d], me.at_seq(target, me.c))

    def kv_start(d, _):
        kv_copy(d).start()
        return 0

    lax.fori_loop(1, 8, kv_start, 0)

    for k in (8, 9):
        loads[k].wait()
    lane = lax.broadcasted_iota(jnp.int32, (128, ROWS), 1)
    slot = lax.broadcasted_iota(jnp.int32, (128, ROWS), 0)
    ids = ids_ref[...]
    weight = score_ref[...] / jnp.sum(score_ref[...], axis=0, keepdims=True)
    routed = jnp.zeros((128, ROWS), F32)
    shares = jnp.zeros((128, ROWS), F32)
    for q in range(4):
        pair = l if q < 2 else 1 - l
        match = ids == 4 * z + 2 * pair + q % 2
        here = lax.div(slot, CAP) == q
        routed = jnp.where(here, jnp.sum(jnp.where(match, 1.0, 0.0), axis=0, keepdims=True), routed)
        shares = jnp.where(here, jnp.sum(jnp.where(match, weight, 0.0), axis=0, keepdims=True), shares)
    earlier = jnp.where(slot < lane, 1.0, 0.0).astype(BF16)
    rank = dot(routed.astype(BF16), earlier)
    chosen = (routed > 0.5) & (rank == lax.rem(slot, CAP).astype(F32))
    table[...] = jnp.where(chosen, 1.0, 0.0).astype(BF16)
    spread_all = jnp.where(chosen, shares, 0.0).T
    spread_high = spread_all.astype(BF16)
    spread[0] = spread_high
    spread[1] = (spread_all - spread_high.astype(F32)).astype(BF16)
    acc[...] = jnp.zeros_like(acc)
    ssq[...] = jnp.zeros_like(ssq)
    for cp in loads[5:8] + loads[10:]:
        cp.wait()

    def kv_wait(d, _):
        ref = kv.at[lax.rem(me.yh + 8 - d, 8), me.c]
        remote(ref, ref, kv_send.at[d], kv_recv.at[d], me.at_other_core()).wait_recv()
        return 0

    lax.fori_loop(1, 8, kv_wait, 0)
    ref = kv.at[:, me.c]
    core_copy = remote(ref, ref, core_send, core_recv, me.at_other_core())
    core_copy.start()

    def weight_copy(k):
        j, ab = lax.div(k, 2), lax.rem(k, 2)
        at = me.z_step(ab * (2 * j + 1) - j)
        cols = pl.ds(pl.multiple_of(at * 256, 256), 256)
        return remote(
            wcat.at[:, 0, :, cols], wcat.at[:, 1, :, cols], wx_send.at[j, ab], wx_recv.at[j, ab], me.at_other_h()
        )

    def down_copy(h, c):
        dst = wdown.at[:, :, c, lax.rem(1 - me.h + h, 2), :, pl.ds(256, 256)]
        k = 2 * h + c
        return remote(wd_hbm.at[:, :, h, c], dst, wy_send.at[k], wy_recv.at[k], me.at_other_h())

    ref = kv.at[:, 1 - me.c]
    remote(ref, ref, core_send, core_recv, me.at_other_core()).wait_recv()

    keys = kv[:, :, 0].reshape(16 * ROWS, HD)
    scores = dot_t(q_ref[...], keys) * HD ** (-0.5)
    key_pos = lax.broadcasted_iota(jnp.int32, (ROWS, 16 * ROWS), 1)
    query_pos = lax.broadcasted_iota(jnp.int32, (ROWS, 16 * ROWS), 0) + s * ROWS
    scores = jnp.where(query_pos >= key_pos, scores, NEG_FILL)
    row_max = jnp.max(scores, axis=1, keepdims=True)
    exp_weights = jnp.exp(scores - row_max)
    row_total = jnp.sum(exp_weights, axis=1, keepdims=True)
    values = kv[:, :, 1].reshape(16 * ROWS, HD)
    head[...] = (dot(exp_weights.astype(BF16), values) / row_total).astype(BF16)

    def head_share(target):
        return dot(head[...], proj[:, pl.ds(pl.multiple_of(target * 256, 256), 256)])

    head_sum = ZSum(me, head_share, sum_in, sum_out, ps_send, ps_recv)
    x_ring = ZRing(me, xcols, xz_send, xz_recv)
    parts = head_sum.run(lambda k: weight_copy(jnp.int32(k)).start())

    def swap(half):
        return remote(
            partial.at[half, 1 - l], partial_in.at[half], pl_send.at[half], pl_recv.at[half], me.at_other_l()
        )

    for half in range(2):
        partial[half, 0] = parts[half][:, 0:HD]
        partial[half, 1] = parts[half][:, HD:]
        swap(half).start()
    for half in range(2):
        rows = pl.ds(half * HALF, HALF)
        swap(half).wait_recv()
        projected = partial[half, l] + partial_in[half]
        attn_ref[rows, :] = projected.astype(BF16)
        xcols[z, rows, :] = (projected + res_ref[rows, :].astype(F32)).astype(BF16)
        x_ring.start(half)

    xs_gather = GroupGather(me, xs, xs_send, xs_recv)

    def x_swap(j):
        return remote(
            sx.at[j],
            xs.at[j, me.y, me.c, :, :, pl.ds(pl.multiple_of(l * HD, HD), HD)],
            xl_send.at[j],
            xl_recv.at[j],
            me.at_other_l(),
        )

    def dispatch(t, _):
        @pl.when(t < STEPS)
        def _():
            low, high = x_ring.step(t)
            for ab, at in enumerate((low, high)):
                picked = dot(table[...], xcols[at]).astype(BF16)
                sx[t, ab] = picked[64:]
                xs[t, me.y, me.c, ab, :, pl.ds(pl.multiple_of(l * HD, HD), HD)] = picked[:64]
            x_swap(t).start()
            weight_copy(t + STEPS).start()

        @pl.when((t >= 1) & (t < STEPS + 1))
        def _():
            j = t - 1
            ref = xs.at[j, me.y, me.c, :, :, pl.ds(pl.multiple_of((1 - l) * HD, HD), HD)]
            remote(ref, ref, xl_send.at[j], xl_recv.at[j], me.at_other_l()).wait_recv()
            xs_gather.a(j)

        @pl.when((t >= 2) & (t < STEPS + 2))
        def _():
            xs_gather.c(t - 2)

        @pl.when((t >= 3) & (t < STEPS + 3))
        def _():
            xs_gather.d(t - 3)

        for h in range(2):
            for c in range(2):

                @pl.when(t == STEPS + 2 * h + c)
                def _():
                    down_copy(h, c).start()

        @pl.when(t >= 4)
        def _():
            j = t - 4
            xs_gather.e(j)
            for ab in range(2):
                at = me.z_step(j + 1) if ab else me.z_step(-j)
                cols = pl.ds(pl.multiple_of(at * 256, 256), 256)
                ref = wcat.at[:, 1, :, cols]
                remote(ref, ref, wx_send.at[j, ab], wx_recv.at[j, ab], me.at_other_h()).wait_recv()
                for i in range(2):
                    x = xs[j, :, :, ab, pl.ds(i * CAP, CAP), :].reshape(8 * CAP, 256)
                    for own in range(2):
                        acc[i, own] += dot_t(x, wcat[i, own, :, cols])
                    wide = x.astype(F32)
                    square = wide * wide
                    ssq[i] += square[:, :128] + square[:, 128:]

        return 0

    lax.fori_loop(0, STEPS + 4, dispatch, 0)

    hid_gather = GroupGather(me, hid, hid_send, hid_recv)
    for k in range(CHUNKS):
        i = k // 2
        rows = pl.ds((k % 2) * ROWS, ROWS)
        scale = lax.rsqrt(jnp.sum(ssq[i, rows, :], axis=1, keepdims=True) * (1.0 / D) + NORM_EPS)
        made = []
        for own in range(2):
            gate = acc[i, own, rows, 0:64] * scale
            up = acc[i, own, rows, 64:128] * scale
            made.append((gate / (1.0 + jnp.exp(-gate)) * up).astype(BF16))
        hid[k, me.y, me.c] = jnp.concatenate(made, axis=1).reshape(2, HALF, 128)
        hid_gather.a(k)

    def down_ready(h, c):
        dst = wdown.at[:, :, c, lax.rem(me.h + h, 2), :, pl.ds(256, 256)]
        k = 2 * h + c
        remote(dst, dst, wy_send.at[k], wy_recv.at[k], me.at_other_h()).wait_recv()

    def down(k):
        i = k // 2
        total = jnp.zeros((ROWS, 512), F32)
        for y in range(4):
            for c in range(2):
                total += dot(hid[k, y, c].reshape(ROWS, 128), wdown[i, y, c].reshape(128, 512))
        made = total.astype(BF16)
        blocks = pl.ds((k % 2) * 4, 4)
        for side in range(2):
            for half in range(2):
                at = side * 256 + half * HD
                prod[blocks, half, pl.ds(i * CAP, CAP), side * HD:(side + 1) * HD] = made[
                    :, at:at + HD
                ].reshape(4, CAP, HD)

    for t in range(CHUNKS + 2):
        if t < CHUNKS:
            hid_gather.c(t)
        if 1 <= t < CHUNKS + 1:
            hid_gather.d(t - 1)
        if t >= 2:
            hid_gather.e(t - 2)
            if t == 2:
                for h in range(2):
                    for c in range(2):
                        down_ready(h, c)
            down(t - 2)

    def back_copy(d):
        other = lax.rem(block + lax.div(d, 2), 8)
        odd = lax.rem(d, 2)
        return remote(
            prod.at[other, lax.rem(l + d, 2)],
            ret.at[block, pl.ds(pl.multiple_of(odd * 64, 64), 64), :],
            ret_send.at[d],
            ret_recv.at[d],
            group_peer(d),
        )

    def back_start(d, _):
        back_copy(d).start()
        return 0

    lax.fori_loop(1, 16, back_start, 0)
    ret[block, 0:64, :] = prod[block, l]

    def back_wait(d, _):
        odd = lax.rem(d, 2)
        other = lax.rem(block + 8 - lax.div(d, 2), 8)
        ref = ret.at[other, pl.ds(pl.multiple_of(odd * 64, 64), 64), :]
        remote(ref, ref, ret_send.at[d], ret_recv.at[d], me.at_other_l()).wait_recv()
        return 0

    lax.fori_loop(1, 16, back_wait, 0)

    def expert_share(target):
        at = lax.div(target, 4) * 2 + lax.rem(target, 2)
        side = lax.rem(lax.div(target, 2) + me.h, 2)
        returned = ret[at, :, pl.ds(pl.multiple_of(side * HD, HD), HD)]
        return dot(spread[0], returned) + dot(spread[1], returned)

    expert_sum = ZSum(me, expert_share, ring_in, ring_out, rz_send, rz_recv)
    parts = expert_sum.run()
    for half in range(2):
        out_ref[pl.ds(half * HALF, HALF), :] = parts[half].astype(BF16)

    core_copy.wait_send()
    head_sum.finish()
    x_ring.finish()
    expert_sum.finish()
    for half in range(2):
        swap(half).wait_send()
    for h in range(2):
        for c in range(2):
            down_copy(h, c).wait_send()

    def kv_sent(d, _):
        kv_copy(d).wait_send()
        return 0

    def back_sent(d, _):
        back_copy(d).wait_send()
        return 0

    def xs_sent(j, _):
        x_swap(j).wait_send()
        xs_gather.finish(j)
        weight_copy(2 * j).wait_send()
        weight_copy(2 * j + 1).wait_send()
        return 0

    def hid_sent(j, _):
        hid_gather.finish(j)
        return 0

    lax.fori_loop(1, 8, kv_sent, 0)
    lax.fori_loop(1, 16, back_sent, 0)
    lax.fori_loop(0, STEPS, xs_sent, 0)
    lax.fori_loop(0, CHUNKS, hid_sent, 0)


def per_device(
    queries, key_states, value_states, residual, out_proj, norm_gain,
    expert_ids, gate_scores, w_gate, w_up, w_down,
):
    vmem = pl.BlockSpec(memory_space=pltpu.VMEM)
    hbm = pl.BlockSpec(memory_space=pltpu.MemorySpace.HBM)
    dma = pltpu.SemaphoreType.DMA
    out = jax.ShapeDtypeStruct((ROWS, HD), BF16)
    scratch = [
        pltpu.VMEM((ROWS, HD), BF16),
        pltpu.VMEM((ROWS, HD), BF16),
        pltpu.VMEM((1, D), F32),
        pltpu.VMEM((8, ROWS), jnp.int32),
        pltpu.VMEM((8, ROWS), F32),
        pltpu.VMEM((8, 2, 2, ROWS, HD), BF16),
        pltpu.VMEM((HD, D), BF16),
        pltpu.VMEM((ROWS, HD), BF16),
        pltpu.VMEM((2, 2, HALF, HD), F32),
        pltpu.VMEM((2, HALF, HD), F32),
        pltpu.VMEM((NZ, ROWS, HD), BF16),
        pltpu.VMEM((STEPS, 4, 2, 2, 64, 256), BF16),
        pltpu.VMEM((STEPS, 2, 64, HD), BF16),
        pltpu.VMEM((2, 64, D), BF16),
        pltpu.VMEM((2, 64, D), BF16),
        pltpu.VMEM((2, 2, 128, D), BF16),
        pltpu.VMEM((2, 4, 2, 2, 64, 512), BF16),
        pltpu.VMEM((2, 2, 256, 128), F32),
        pltpu.VMEM((2, 256, 128), F32),
        pltpu.VMEM((CHUNKS, 4, 2, 2, HALF, 128), BF16),
        pltpu.VMEM((8, 2, 64, 256), BF16),
        pltpu.VMEM((8, 128, 256), BF16),
        pltpu.VMEM((128, ROWS), BF16),
        pltpu.VMEM((2, ROWS, 128), BF16),
        pltpu.VMEM((2, 9, 2, HALF, 256), BF16),
        pltpu.VMEM((2, 9, 2, HALF, 256), BF16),
        pltpu.VMEM((2, 9, 2, HALF, HD), BF16),
        pltpu.VMEM((2, 9, 2, HALF, HD), BF16),
        dma((14,)),
        dma((8,)), dma((8,)),
        dma, dma,
        dma((STEPS, 2)), dma((STEPS, 2)),
        dma((4,)), dma((4,)),
        dma((2, 9, 2)), dma((2, 9, 2)),
        dma((2,)), dma((2,)),
        dma((2, 9, 2)), dma((2, 9, 2)),
        dma((STEPS,)), dma((STEPS,)),
        dma((STEPS, 5)), dma((STEPS, 5)),
        dma((CHUNKS, 5)), dma((CHUNKS, 5)),
        dma((16,)), dma((16,)),
        dma((2, 9, 2)), dma((2, 9, 2)),
    ]
    return pl.pallas_call(
        kernel,
        out_shape=(out, out),
        in_specs=[hbm] * 11,
        out_specs=(vmem, vmem),
        scratch_shapes=scratch,
        compiler_params=pltpu.CompilerParams(
            collective_id=0, has_side_effects=True, vmem_limit_bytes=63 * 2**20
        ),
        cost_estimate=pl.CostEstimate(flops=2 * 10**9, bytes_accessed=8 * 10**6, transcendentals=10**6),
        name="layer",
    )(
        queries, residual, norm_gain.reshape(1, D), expert_ids.T, gate_scores.T,
        key_states, value_states, out_proj, w_gate, w_up,
        w_down.reshape(2, 4, 2, 2, 64, 256),
    )


def solution(mesh):
    placed = (
        P("seq", "exp"),
        P("seq", None),
        P("seq", None),
        P("seq", "exp"),
        P("exp", None),
        P(),
        P("seq", None),
        P("seq", None),
        P("exp", "seq", None),
        P("exp", "seq", None),
        P("exp", None, "seq"),
    )
    return jax.shard_map(
        per_device,
        mesh=mesh,
        in_specs=placed,
        out_specs=(P("seq", "exp"), P("seq", "exp")),
        check_vma=False,
    )
```

```python
import jax
import jax.numpy as jnp
from jax import lax
from jax.experimental import pallas as pl
from jax.experimental.pallas import tpu as pltpu
from jax.sharding import PartitionSpec as P

MESH = pl.DeviceIdType.MESH
BF16 = jnp.bfloat16
F32 = jnp.float32
NEG_FILL = -1e30
NORM_EPS = 1e-06
D = 4096
HD = 128
ROWS = 128
NZ = 16
STEPS = 8
CAP = 32
CHUNKS = 4
HALF = 64


def dot(a, b):
    return jnp.dot(a, b, preferred_element_type=F32)


def dot_t(a, b):
    return lax.dot_general(a, b, (((1,), (1,)), ((), ())), preferred_element_type=F32)


def remote(src, dst, send_sem, recv_sem, device):
    return pltpu.make_async_remote_copy(
        src_ref=src,
        dst_ref=dst,
        send_sem=send_sem,
        recv_sem=recv_sem,
        device_id=device,
        device_id_type=MESH,
    )


class Place:
    def __init__(self):
        self.s = lax.axis_index("seq")
        self.e = lax.axis_index("exp")
        self.yh = lax.div(self.s, 2)
        self.c = lax.rem(self.s, 2)
        self.y = lax.div(self.s, 4)
        self.h = lax.rem(self.yh, 2)
        self.z = lax.div(self.e, 2)
        self.l = lax.rem(self.e, 2)

    def seq_of(self, y, h, c):
        return (y * 2 + h) * 2 + c

    def y_step(self, k):
        return lax.rem(self.y + k + 4, 4)

    def z_step(self, k):
        return lax.rem(self.z + k + 32, NZ)

    def at_seq(self, yh, c):
        return (yh * 2 + c, self.e)

    def at_y(self, k):
        return (self.seq_of(self.y_step(k), self.h, self.c), self.e)

    def at_other_h(self):
        return (self.seq_of(self.y, 1 - self.h, self.c), self.e)

    def at_other_core(self):
        return (self.seq_of(self.y, self.h, 1 - self.c), self.e)

    def at_z(self, k):
        return (self.s, self.z_step(k) * 2 + self.l)

    def at_other_l(self):
        return (self.s, self.z * 2 + 1 - self.l)


class GroupGather:
    def __init__(self, me, buf, send, recv):
        self.me, self.buf, self.send, self.recv = me, buf, send, recv

    def copy(self, j, k, ref, device):
        return remote(ref, ref, self.send.at[j, k], self.recv.at[j, k], device)

    def push(self, j, k):
        me = self.me
        if k < 2:
            return self.copy(j, k, self.buf.at[j, me.y, me.c], me.at_y(1 - 2 * k))
        if k < 4:
            way = 5 - 2 * k
            return self.copy(j, k, self.buf.at[j, me.y_step(-way), me.c, k - 2], me.at_y(way))
        return self.copy(j, k, self.buf.at[j, :, me.c], me.at_other_core())

    def arrived(self, j, k):
        me = self.me
        if k < 2:
            ref = self.buf.at[j, me.y_step(2 * k - 1), me.c]
        elif k < 4:
            ref = self.buf.at[j, me.y_step(2), me.c, k - 2]
        else:
            ref = self.buf.at[j, :, 1 - me.c]
        self.copy(j, k, ref, me.at_other_core()).wait_recv()

    def a(self, j):
        self.push(j, 0).start()
        self.push(j, 1).start()

    def c(self, j):
        for k in range(2):
            self.arrived(j, k)
            self.push(j, 2 + k).start()

    def d(self, j):
        self.arrived(j, 2)
        self.arrived(j, 3)
        self.push(j, 4).start()

    def e(self, j):
        self.arrived(j, 4)

    def finish(self, j):
        for k in range(5):
            self.push(j, k).wait_send()


class ZRing:
    def __init__(self, me, buf, send, recv):
        self.me, self.buf, self.send, self.recv = me, buf, send, recv

    def copy(self, way, k, block, hops):
        ref = self.buf.at[block]
        return remote(
            ref, ref, self.send.at[way, k], self.recv.at[way, k], self.me.at_z(hops - 2 * way * hops)
        )

    def up(self, k, hops=2):
        return self.copy(0, k, self.me.z_step(hops - k), hops)

    def down(self, k, hops=2):
        return self.copy(1, k, self.me.z_step(k - hops), hops)

    def start(self):
        for hops in (1, 2):
            self.down(hops, hops).start()
            self.up(hops, hops).start()

    def step(self, j):
        low, high = self.me.z_step(-j), self.me.z_step(j + 1)
        self.copy(1, j + 1, high, 2).wait_recv()

        @pl.when(j < STEPS - 2)
        def _():
            self.down(j + 3).start()

        @pl.when(j >= 1)
        def _():
            self.copy(0, j, low, 2).wait_recv()

            @pl.when(j < STEPS - 2)
            def _():
                self.up(j + 2).start()

        return low, high

    def finish(self):
        for hops in (1, 2):
            self.down(hops, hops).wait_send()
            self.up(hops, hops).wait_send()

        def one(k, _):
            self.down(k).wait_send()

            @pl.when(k < STEPS)
            def _():
                self.up(k).wait_send()

            return 0

        lax.fori_loop(3, STEPS + 1, one, 0)


class ZSum:
    def __init__(self, me, share, inbox, outbox, send, recv):
        self.me, self.share = me, share
        self.inbox, self.outbox, self.send, self.recv = inbox, outbox, send, recv

    def copy(self, way, k, hops=2):
        return remote(
            self.outbox.at[way, k],
            self.inbox.at[way, k],
            self.send.at[way, k],
            self.recv.at[way, k],
            self.me.at_z(hops - 2 * way * hops),
        )

    def step(self, k, beside, first=False, hops=(2, 2)):
        places = [(0, 8 - k, self.me.z_step(8 - k))]
        if len(hops) > 1:
            places.append((1, 7 - k, self.me.z_step(k - 7)))
        shares = [self.share(target) for _, _, target in places]
        for (way, far, _), part in zip(places, shares):
            if not first:
                self.copy(way, far + 2).wait_recv()
                part = part + self.inbox[way, far + 2].astype(F32)
            self.outbox[way, far] = part.astype(BF16)
            self.copy(way, far, hops[way]).start()
        beside(k)

    def run(self, beside=lambda k: None):
        self.step(0, beside, first=True)
        self.step(1, beside, first=True)

        def one(k, _):
            self.step(k, beside)
            return 0

        lax.fori_loop(2, 6, one, 0)
        self.step(6, beside, hops=(2, 1))
        self.step(7, beside, hops=(1,))
        total = self.share(self.me.z)
        for k in (2, 1):
            for way in (1, 0):
                self.copy(way, k).wait_recv()
                total = total + self.inbox[way, k].astype(F32)
        return total

    def finish(self):
        def one(k, _):
            self.copy(0, k).wait_send()

            @pl.when(k < 8)
            def _():
                self.copy(1, k).wait_send()

            return 0

        lax.fori_loop(1, 9, one, 0)


def kernel(
    q_hbm, res_hbm, gain_hbm, ids_hbm, score_hbm,
    key_hbm, val_hbm, proj_hbm, wg_hbm, wu_hbm, wd_hbm,
    attn_ref, out_ref,
    q_ref, res_ref, gain_ref, ids_ref, score_ref,
    kv, proj, staged, heads, xcols, xs, sx,
    wg, wu, wcat, wdown, acc, ssq, hid, prod, ret, table, spread,
    sum_in, sum_out, ring_in, ring_out,
    local_sem, kv_send, kv_recv, core_send, core_recv, wx_send, wx_recv, wy_send, wy_recv,
    proj_sem, pj_send, pj_recv, pc_send, pc_recv, hd_send, hd_recv, ps_send, ps_recv, xz_send, xz_recv, xl_send, xl_recv,
    xs_send, xs_recv, hid_send, hid_recv, ret_send, ret_recv, rz_send, rz_recv,
):
    me = Place()
    s, z, l = me.s, me.z, me.l
    block = me.y * 2 + me.c

    group = pl.multiple_of(lax.div(z, 4) * HD, HD)
    loads = [
        pltpu.make_async_copy(src, dst, local_sem.at[k])
        for k, (src, dst) in enumerate(
            [
                (key_hbm.at[:, pl.ds(group, HD)], kv.at[me.yh, me.c, 0]),
                (val_hbm.at[:, pl.ds(group, HD)], kv.at[me.yh, me.c, 1]),
                (gain_hbm, gain_ref),
                (wg_hbm, wg),
                (wu_hbm, wu),
                (q_hbm, q_ref.at[0]),
                (res_hbm, res_ref),
                (ids_hbm, ids_ref),
                (score_hbm, score_ref),
            ]
        )
    ]
    for h in range(2):
        for c in range(2):
            dst = wdown.at[0, :, :, c, lax.rem(me.h + h, 2)]
            loads.append(pltpu.make_async_copy(wd_hbm.at[:, :, h, c], dst, local_sem.at[9 + 2 * h + c]))
    for cp in loads:
        cp.start()

    def proj_cols(at, half):
        return proj_hbm.at[:, pl.ds(pl.multiple_of(at * 256 + half * HD, HD), HD)]

    def proj_load(at):
        return pltpu.make_async_copy(
            proj_cols(at, l), proj.at[0, lax.div(at, 2), lax.rem(at, 2)], proj_sem.at[at]
        )

    def proj_stage(k):
        return pltpu.make_async_copy(proj_cols(2 * k + me.c, 1 - l), staged.at[k], proj_sem.at[NZ + k])

    proj_copy = remote(staged, proj.at[1, :, me.c], pj_send, pj_recv, me.at_other_l())

    def proj_load_start(at, _):
        proj_load(at).start()
        return 0

    def proj_stage_start(k, _):
        proj_stage(k).start()
        return 0

    lax.fori_loop(0, 8, proj_stage_start, 0)
    lax.fori_loop(0, NZ, proj_load_start, 0)

    def seq_peer(d):
        return (lax.rem(s + d, 16), me.e)

    def group_peer(d):
        other = lax.rem(block + lax.div(d, 2), 8)
        place = me.seq_of(lax.div(other, 2), me.h, lax.rem(other, 2))
        return (place, z * 2 + lax.rem(l + d, 2))

    barrier = pltpu.get_barrier_semaphore()

    def greet_seq(d, _):
        pl.semaphore_signal(barrier, inc=1, device_id=seq_peer(d), device_id_type=MESH)
        return 0

    def greet_group(d, _):
        pl.semaphore_signal(barrier, inc=1, device_id=group_peer(2 * d + 1), device_id_type=MESH)
        return 0

    lax.fori_loop(1, 16, greet_seq, 0)
    lax.fori_loop(0, 8, greet_group, 0)
    for k in (1, -1, 2, -2):
        pl.semaphore_signal(barrier, inc=1, device_id=me.at_z(k), device_id_type=MESH)

    loads[2].wait()
    loads[3].wait()
    loads[4].wait()
    gain = gain_ref[...]
    for at in range(NZ):
        cols = slice(at * 256, (at + 1) * 256)
        for i in range(2):
            wcat[at, 0, i, 0:64, :] = (wg[i, :, cols].astype(F32) * gain[:, cols]).astype(BF16)
            wcat[at, 0, i, 64:128, :] = (wu[i, :, cols].astype(F32) * gain[:, cols]).astype(BF16)

    loads[0].wait()
    loads[1].wait()
    pl.semaphore_wait(barrier, 15 + 8 + 4)

    def kv_copy(d):
        ref = kv.at[me.yh, me.c]
        target = lax.rem(me.yh + d, 8)
        return remote(ref, ref, kv_send.at[d], kv_recv.at[d], me.at_seq(target, me.c))

    q_copy = remote(q_hbm, q_ref.at[1], hd_send, hd_recv, me.at_other_l())
    q_copy.start()

    def kv_start(d, _):
        kv_copy(d).start()
        return 0

    lax.fori_loop(1, 8, kv_start, 0)

    def proj_staged(k, _):
        proj_stage(k).wait()
        return 0

    lax.fori_loop(0, 8, proj_staged, 0)
    proj_copy.start()
    def weight_copy(k):
        j, ab = lax.div(k, 2), lax.rem(k, 2)
        at = me.z_step(ab * (2 * j + 1) - j)
        return remote(
            wcat.at[at, 0], wcat.at[at, 1], wx_send.at[j, ab], wx_recv.at[j, ab], me.at_other_h()
        )

    def down_copy(h, c):
        dst = wdown.at[1, :, :, c, lax.rem(1 - me.h + h, 2)]
        k = 2 * h + c
        return remote(wd_hbm.at[:, :, h, c], dst, wy_send.at[k], wy_recv.at[k], me.at_other_h())


    for k in (7, 8):
        loads[k].wait()
    lane = lax.broadcasted_iota(jnp.int32, (128, ROWS), 1)
    slot = lax.broadcasted_iota(jnp.int32, (128, ROWS), 0)
    ids = ids_ref[...]
    weight = score_ref[...] / jnp.sum(score_ref[...], axis=0, keepdims=True)
    routed = jnp.zeros((128, ROWS), F32)
    shares = jnp.zeros((128, ROWS), F32)
    for q in range(4):
        pair = l if q < 2 else 1 - l
        match = ids == 4 * z + 2 * pair + q % 2
        here = lax.div(slot, CAP) == q
        routed = jnp.where(here, jnp.sum(jnp.where(match, 1.0, 0.0), axis=0, keepdims=True), routed)
        shares = jnp.where(here, jnp.sum(jnp.where(match, weight, 0.0), axis=0, keepdims=True), shares)
    earlier = jnp.where(slot < lane, 1.0, 0.0).astype(BF16)
    rank = dot(routed.astype(BF16), earlier)
    chosen = (routed > 0.5) & (rank == lax.rem(slot, CAP).astype(F32))
    table[...] = jnp.where(chosen, 1.0, 0.0).astype(BF16)
    spread_all = jnp.where(chosen, shares, 0.0).T
    spread_high = spread_all.astype(BF16)
    spread[0] = spread_high
    spread[1] = (spread_all - spread_high.astype(F32)).astype(BF16)
    acc[...] = jnp.zeros_like(acc)
    ssq[...] = jnp.zeros_like(ssq)
    for cp in loads[5:7] + loads[9:]:
        cp.wait()

    def proj_loaded(at, _):
        proj_load(at).wait()
        return 0

    lax.fori_loop(0, NZ, proj_loaded, 0)

    def kv_wait(d, _):
        ref = kv.at[lax.rem(me.yh + 8 - d, 8), me.c]
        remote(ref, ref, kv_send.at[d], kv_recv.at[d], me.at_other_core()).wait_recv()
        return 0

    lax.fori_loop(1, 8, kv_wait, 0)
    ref = kv.at[:, me.c]
    core_copy = remote(ref, ref, core_send, core_recv, me.at_other_core())
    core_copy.start()

    proj_copy.wait_recv()
    ref = proj.at[1, :, me.c]
    proj_core = remote(ref, ref, pc_send, pc_recv, me.at_other_core())
    proj_core.start()

    weight_copy(jnp.int32(0)).start()
    weight_copy(jnp.int32(1)).start()
    ref = kv.at[:, 1 - me.c]
    remote(ref, ref, core_send, core_recv, me.at_other_core()).wait_recv()

    q_copy.wait_recv()
    keys = kv[:, :, 0].reshape(16 * ROWS, HD)
    values = kv[:, :, 1].reshape(16 * ROWS, HD)
    key_pos = lax.broadcasted_iota(jnp.int32, (ROWS, 16 * ROWS), 1)
    query_pos = lax.broadcasted_iota(jnp.int32, (ROWS, 16 * ROWS), 0) + s * ROWS
    for k in range(2):
        scores = dot_t(q_ref[k], keys) * HD ** (-0.5)
        scores = jnp.where(query_pos >= key_pos, scores, NEG_FILL)
        row_max = jnp.max(scores, axis=1, keepdims=True)
        exp_weights = jnp.exp(scores - row_max)
        row_total = jnp.sum(exp_weights, axis=1, keepdims=True)
        heads[k] = (dot(exp_weights.astype(BF16), values) / row_total).astype(BF16)
    ref = proj.at[1, :, 1 - me.c]
    remote(ref, ref, pc_send, pc_recv, me.at_other_core()).wait_recv()

    def head_share(target):
        at, odd = lax.div(target, 2), lax.rem(target, 2)
        return dot(heads[0], proj[0, at, odd]) + dot(heads[1], proj[1, at, odd])

    head_sum = ZSum(me, head_share, sum_in, sum_out, ps_send, ps_recv)
    projected = head_sum.run(lambda k: weight_copy(k + jnp.int32(2)).start())
    attn_ref[...] = projected.astype(BF16)
    xcols[z] = (projected + res_ref[...].astype(F32)).astype(BF16)
    x_ring = ZRing(me, xcols, xz_send, xz_recv)
    x_ring.start()

    xs_gather = GroupGather(me, xs, xs_send, xs_recv)

    def x_swap(j):
        return remote(
            sx.at[j],
            xs.at[j, me.y, me.c, :, :, pl.ds(pl.multiple_of(l * HD, HD), HD)],
            xl_send.at[j],
            xl_recv.at[j],
            me.at_other_l(),
        )

    def dispatch(t, _):
        @pl.when(t < STEPS)
        def _():
            low, high = x_ring.step(t)
            for ab, at in enumerate((low, high)):
                picked = dot(table[...], xcols[at]).astype(BF16)
                sx[t, ab] = picked[64:]
                xs[t, me.y, me.c, ab, :, pl.ds(pl.multiple_of(l * HD, HD), HD)] = picked[:64]
            x_swap(t).start()

            @pl.when(t < 6)
            def _():
                weight_copy(t + 10).start()

        @pl.when((t >= 1) & (t < STEPS + 1))
        def _():
            j = t - 1
            ref = xs.at[j, me.y, me.c, :, :, pl.ds(pl.multiple_of((1 - l) * HD, HD), HD)]
            remote(ref, ref, xl_send.at[j], xl_recv.at[j], me.at_other_l()).wait_recv()
            xs_gather.a(j)

        @pl.when((t >= 2) & (t < STEPS + 2))
        def _():
            xs_gather.c(t - 2)

        @pl.when((t >= 3) & (t < STEPS + 3))
        def _():
            xs_gather.d(t - 3)

        for h in range(2):
            for c in range(2):

                @pl.when(t == 6 + 2 * h + c)
                def _():
                    down_copy(h, c).start()

        @pl.when(t >= 4)
        def _():
            j = t - 4
            xs_gather.e(j)
            for ab in range(2):
                at = me.z_step(j + 1) if ab else me.z_step(-j)
                ref = wcat.at[at, 1]
                remote(ref, ref, wx_send.at[j, ab], wx_recv.at[j, ab], me.at_other_h()).wait_recv()
                for i in range(2):
                    x = xs[j, :, :, ab, pl.ds(i * CAP, CAP), :].reshape(8 * CAP, 256)
                    for own in range(2):
                        acc[i, own] += dot_t(x, wcat[at, own, i])
                    wide = x.astype(F32)
                    square = wide * wide
                    ssq[i] += square[:, :128] + square[:, 128:]

        return 0

    lax.fori_loop(0, STEPS + 4, dispatch, 0)

    hid_gather = GroupGather(me, hid, hid_send, hid_recv)
    for k in range(CHUNKS):
        i = k % 2
        rows = pl.ds((k // 2) * ROWS, ROWS)
        scale = lax.rsqrt(jnp.sum(ssq[i, rows, :], axis=1, keepdims=True) * (1.0 / D) + NORM_EPS)
        made = []
        for own in range(2):
            gate = acc[i, own, rows, 0:64] * scale
            up = acc[i, own, rows, 64:128] * scale
            made.append((gate / (1.0 + jnp.exp(-gate)) * up).astype(BF16))
        hid[k, me.y, me.c] = jnp.concatenate(made, axis=1).reshape(2, HALF, 128)
        hid_gather.a(k)

    def down_ready(h, c):
        dst = wdown.at[1, :, :, c, lax.rem(me.h + h, 2)]
        k = 2 * h + c
        remote(dst, dst, wy_send.at[k], wy_recv.at[k], me.at_other_h()).wait_recv()

    def down(k):
        i = k % 2
        totals = [jnp.zeros((ROWS, 256), F32)] * 2
        for y in range(4):
            for c in range(2):
                rows = hid[k, y, c].reshape(ROWS, 128)
                for side in range(2):
                    totals[side] += dot(rows, wdown[side, i, y, c].reshape(128, 256))
        blocks = pl.ds((k // 2) * 4, 4)
        for side in range(2):
            for half in range(2):
                made = totals[side][:, half * HD:(half + 1) * HD].astype(BF16)
                prod[blocks, half, pl.ds(i * CAP, CAP), side * HD:(side + 1) * HD] = made.reshape(4, CAP, HD)

    def back_copy(d):
        other = lax.rem(block + lax.div(d, 2), 8)
        odd = lax.rem(d, 2)
        return remote(
            prod.at[other, lax.rem(l + d, 2)],
            ret.at[block, pl.ds(pl.multiple_of(odd * 64, 64), 64), :],
            ret_send.at[d],
            ret_recv.at[d],
            group_peer(d),
        )

    def back_start(target, _):
        for odd in range(2):
            d = 2 * lax.rem(target + 8 - block, 8) + odd

            @pl.when(d != 0)
            def _():
                back_copy(d).start()

        return 0

    for t in range(CHUNKS + 2):
        if t < CHUNKS:
            hid_gather.c(t)
        if 1 <= t < CHUNKS + 1:
            hid_gather.d(t - 1)
        if t >= 2:
            hid_gather.e(t - 2)
            if t == 2:
                for h in range(2):
                    for c in range(2):
                        down_ready(h, c)
            down(t - 2)
            if t == 3:
                lax.fori_loop(0, 4, back_start, 0)
            if t == 5:
                lax.fori_loop(4, 8, back_start, 0)

    ret[block, 0:64, :] = prod[block, l]

    def back_wait(d, _):
        odd = lax.rem(d, 2)
        other = lax.rem(block + 8 - lax.div(d, 2), 8)
        ref = ret.at[other, pl.ds(pl.multiple_of(odd * 64, 64), 64), :]
        remote(ref, ref, ret_send.at[d], ret_recv.at[d], me.at_other_l()).wait_recv()
        return 0

    lax.fori_loop(1, 16, back_wait, 0)

    def expert_share(target):
        at = lax.div(target, 4) * 2 + lax.rem(target, 2)
        side = lax.rem(lax.div(target, 2) + me.h, 2)
        returned = ret[at, :, pl.ds(pl.multiple_of(side * HD, HD), HD)]
        return dot(spread[0], returned) + dot(spread[1], returned)

    expert_sum = ZSum(me, expert_share, ring_in, ring_out, rz_send, rz_recv)
    out_ref[...] = expert_sum.run().astype(BF16)

    core_copy.wait_send()
    head_sum.finish()
    x_ring.finish()
    expert_sum.finish()
    proj_core.wait_send()
    q_copy.wait_send()
    for h in range(2):
        for c in range(2):
            down_copy(h, c).wait_send()

    def kv_sent(d, _):
        kv_copy(d).wait_send()
        return 0

    proj_copy.wait_send()

    def back_sent(d, _):
        back_copy(d).wait_send()
        return 0

    def xs_sent(j, _):
        x_swap(j).wait_send()
        xs_gather.finish(j)
        weight_copy(2 * j).wait_send()
        weight_copy(2 * j + 1).wait_send()
        return 0

    def hid_sent(j, _):
        hid_gather.finish(j)
        return 0

    lax.fori_loop(1, 8, kv_sent, 0)
    lax.fori_loop(1, 16, back_sent, 0)
    lax.fori_loop(0, STEPS, xs_sent, 0)
    lax.fori_loop(0, CHUNKS, hid_sent, 0)


def per_device(
    queries, key_states, value_states, residual, out_proj, norm_gain,
    expert_ids, gate_scores, w_gate, w_up, w_down,
):
    vmem = pl.BlockSpec(memory_space=pltpu.VMEM)
    hbm = pl.BlockSpec(memory_space=pltpu.MemorySpace.HBM)
    dma = pltpu.SemaphoreType.DMA
    out = jax.ShapeDtypeStruct((ROWS, HD), BF16)
    scratch = [
        pltpu.VMEM((2, ROWS, HD), BF16),
        pltpu.VMEM((ROWS, HD), BF16),
        pltpu.VMEM((1, D), F32),
        pltpu.VMEM((8, ROWS), jnp.int32),
        pltpu.VMEM((8, ROWS), F32),
        pltpu.VMEM((8, 2, 2, ROWS, HD), BF16),
        pltpu.VMEM((2, 8, 2, HD, HD), BF16),
        pltpu.VMEM((8, HD, HD), BF16),
        pltpu.VMEM((2, ROWS, HD), BF16),
        pltpu.VMEM((NZ, ROWS, HD), BF16),
        pltpu.VMEM((STEPS, 4, 2, 2, 64, 256), BF16),
        pltpu.VMEM((STEPS, 2, 64, HD), BF16),
        pltpu.VMEM((2, 64, D), BF16),
        pltpu.VMEM((2, 64, D), BF16),
        pltpu.VMEM((NZ, 2, 2, 128, 256), BF16),
        pltpu.VMEM((2, 2, 4, 2, 2, 64, 256), BF16),
        pltpu.VMEM((2, 2, 256, 128), F32),
        pltpu.VMEM((2, 256, 128), F32),
        pltpu.VMEM((CHUNKS, 4, 2, 2, HALF, 128), BF16),
        pltpu.VMEM((8, 2, 64, 256), BF16),
        pltpu.VMEM((8, 128, 256), BF16),
        pltpu.VMEM((128, ROWS), BF16),
        pltpu.VMEM((2, ROWS, 128), BF16),
        pltpu.VMEM((2, 9, ROWS, HD), BF16),
        pltpu.VMEM((2, 9, ROWS, HD), BF16),
        pltpu.VMEM((2, 9, ROWS, HD), BF16),
        pltpu.VMEM((2, 9, ROWS, HD), BF16),
        dma((13,)),
        dma((8,)), dma((8,)),
        dma, dma,
        dma((STEPS, 2)), dma((STEPS, 2)),
        dma((4,)), dma((4,)),
        dma((NZ + 8,)),
        dma, dma,
        dma, dma,
        dma, dma,
        dma((2, 9)), dma((2, 9)),
        dma((2, 9)), dma((2, 9)),
        dma((STEPS,)), dma((STEPS,)),
        dma((STEPS, 5)), dma((STEPS, 5)),
        dma((CHUNKS, 5)), dma((CHUNKS, 5)),
        dma((16,)), dma((16,)),
        dma((2, 9)), dma((2, 9)),
    ]
    return pl.pallas_call(
        kernel,
        out_shape=(out, out),
        in_specs=[hbm] * 11,
        out_specs=(vmem, vmem),
        scratch_shapes=scratch,
        compiler_params=pltpu.CompilerParams(
            collective_id=0, has_side_effects=True, vmem_limit_bytes=63 * 2**20
        ),
        cost_estimate=pl.CostEstimate(flops=2 * 10**9, bytes_accessed=8 * 10**6, transcendentals=10**6),
        name="layer",
    )(
        queries, residual, norm_gain.reshape(1, D), expert_ids.T, gate_scores.T,
        key_states, value_states, out_proj, w_gate, w_up,
        w_down.reshape(2, 4, 2, 2, 64, 256),
    )


def solution(mesh):
    placed = (
        P("seq", "exp"),
        P("seq", None),
        P("seq", None),
        P("seq", "exp"),
        P("exp", None),
        P(),
        P("seq", None),
        P("seq", None),
        P("exp", "seq", None),
        P("exp", "seq", None),
        P("exp", None, "seq"),
    )
    return jax.shard_map(
        per_device,
        mesh=mesh,
        in_specs=placed,
        out_specs=(P("seq", "exp"), P("seq", "exp")),
        check_vma=False,
    )
```

```python
import jax
import jax.numpy as jnp
from jax import lax
from jax.experimental import pallas as pl
from jax.experimental.pallas import tpu as pltpu
from jax.sharding import PartitionSpec as P

MESH = pl.DeviceIdType.MESH
BF16 = jnp.bfloat16
F32 = jnp.float32
NEG_FILL = -1e30
NORM_EPS = 1e-06
D = 4096
HD = 128
ROWS = 128
NZ = 16
STEPS = 8
CAP = 32
CHUNKS = 4
HALF = 64


def dot(a, b):
    return jnp.dot(a, b, preferred_element_type=F32)


def dot_t(a, b):
    return lax.dot_general(a, b, (((1,), (1,)), ((), ())), preferred_element_type=F32)


def remote(src, dst, send_sem, recv_sem, device):
    return pltpu.make_async_remote_copy(
        src_ref=src,
        dst_ref=dst,
        send_sem=send_sem,
        recv_sem=recv_sem,
        device_id=device,
        device_id_type=MESH,
    )


class Place:
    def __init__(self):
        self.s = lax.axis_index("seq")
        self.e = lax.axis_index("exp")
        self.yh = lax.div(self.s, 2)
        self.c = lax.rem(self.s, 2)
        self.y = lax.div(self.s, 4)
        self.h = lax.rem(self.yh, 2)
        self.z = lax.div(self.e, 2)
        self.l = lax.rem(self.e, 2)

    def seq_of(self, y, h, c):
        return (y * 2 + h) * 2 + c

    def y_step(self, k):
        return lax.rem(self.y + k + 4, 4)

    def z_step(self, k):
        return lax.rem(self.z + k + 32, NZ)

    def at_seq(self, yh, c):
        return (yh * 2 + c, self.e)

    def at_y(self, k):
        return (self.seq_of(self.y_step(k), self.h, self.c), self.e)

    def at_other_h(self):
        return (self.seq_of(self.y, 1 - self.h, self.c), self.e)

    def at_other_core(self):
        return (self.seq_of(self.y, self.h, 1 - self.c), self.e)

    def at_z(self, k):
        return (self.s, self.z_step(k) * 2 + self.l)

    def at_other_l(self):
        return (self.s, self.z * 2 + 1 - self.l)


class GroupGather:
    def __init__(self, me, buf, send, recv):
        self.me, self.buf, self.send, self.recv = me, buf, send, recv

    def copy(self, j, k, ref, device):
        return remote(ref, ref, self.send.at[j, k], self.recv.at[j, k], device)

    def push(self, j, k):
        me = self.me
        if k < 3:
            return self.copy(j, k, self.buf.at[j, me.y, me.c], me.at_y((1, -1, 2)[k]))
        return self.copy(j, k, self.buf.at[j, :, me.c], me.at_other_core())

    def arrived(self, j, k):
        me = self.me
        if k < 3:
            ref = self.buf.at[j, me.y_step((-1, 1, 2)[k]), me.c]
        else:
            ref = self.buf.at[j, :, 1 - me.c]
        self.copy(j, k, ref, me.at_other_core()).wait_recv()

    def a(self, j):
        for k in (2, 0, 1):
            self.push(j, k).start()

    def d(self, j):
        for k in range(3):
            self.arrived(j, k)
        self.push(j, 3).start()

    def e(self, j):
        self.arrived(j, 3)

    def finish(self, j):
        for k in range(4):
            self.push(j, k).wait_send()


class ZRing:
    def __init__(self, me, buf, send, recv):
        self.me, self.buf, self.send, self.recv = me, buf, send, recv

    def copy(self, way, k, block, hops):
        ref = self.buf.at[block]
        return remote(
            ref, ref, self.send.at[way, k], self.recv.at[way, k], self.me.at_z(hops - 2 * way * hops)
        )

    def up(self, k, hops=2):
        return self.copy(0, k, self.me.z_step(hops - k), hops)

    def down(self, k, hops=2):
        return self.copy(1, k, self.me.z_step(k - hops), hops)

    def start(self):
        for hops in (1, 2):
            self.down(hops, hops).start()
            self.up(hops, hops).start()

    def step(self, j):
        low, high = self.me.z_step(-j), self.me.z_step(j + 1)
        self.copy(1, j + 1, high, 2).wait_recv()

        @pl.when(j < STEPS - 2)
        def _():
            self.down(j + 3).start()

        @pl.when(j >= 1)
        def _():
            self.copy(0, j, low, 2).wait_recv()

            @pl.when(j < STEPS - 2)
            def _():
                self.up(j + 2).start()

        return low, high

    def finish(self):
        for hops in (1, 2):
            self.down(hops, hops).wait_send()
            self.up(hops, hops).wait_send()

        def one(k, _):
            self.down(k).wait_send()

            @pl.when(k < STEPS)
            def _():
                self.up(k).wait_send()

            return 0

        lax.fori_loop(3, STEPS + 1, one, 0)


class ZSum:
    def __init__(self, me, share, inbox, outbox, send, recv):
        self.me, self.share = me, share
        self.inbox, self.outbox, self.send, self.recv = inbox, outbox, send, recv

    def copy(self, way, k, hops=2):
        return remote(
            self.outbox.at[way, k],
            self.inbox.at[way, k],
            self.send.at[way, k],
            self.recv.at[way, k],
            self.me.at_z(hops - 2 * way * hops),
        )

    def step(self, k, beside, first=False, hops=(2, 2)):
        places = [(0, 8 - k, self.me.z_step(8 - k))]
        if len(hops) > 1:
            places.append((1, 7 - k, self.me.z_step(k - 7)))
        shares = [self.share(target) for _, _, target in places]
        for (way, far, _), part in zip(places, shares):
            if not first:
                self.copy(way, far + 2).wait_recv()
                part = part + self.inbox[way, far + 2].astype(F32)
            self.outbox[way, far] = part.astype(BF16)
            self.copy(way, far, hops[way]).start()
        beside(k)

    def run(self, beside=lambda k: None):
        self.step(0, beside, first=True)
        self.step(1, beside, first=True)

        def one(k, _):
            self.step(k, beside)
            return 0

        lax.fori_loop(2, 6, one, 0)
        self.step(6, beside, hops=(2, 1))
        self.step(7, beside, hops=(1,))
        total = self.share(self.me.z)
        for k in (2, 1):
            for way in (1, 0):
                self.copy(way, k).wait_recv()
                total = total + self.inbox[way, k].astype(F32)
        return total

    def finish(self):
        def one(k, _):
            self.copy(0, k).wait_send()

            @pl.when(k < 8)
            def _():
                self.copy(1, k).wait_send()

            return 0

        lax.fori_loop(1, 9, one, 0)


def kernel(
    q_hbm, res_hbm, gain_hbm, ids_hbm, score_hbm,
    key_hbm, val_hbm, proj_hbm, wg_hbm, wu_hbm, wd_hbm,
    attn_ref, out_ref,
    q_ref, res_ref, gain_ref, ids_ref, score_ref,
    kv, proj, staged, heads, xcols, xs, sx,
    wg, wu, wcat, wdown, acc, ssq, hid, prod, ret, table, spread,
    sum_in, sum_out, ring_in, ring_out,
    local_sem, kv_send, kv_recv, core_send, core_recv, wx_send, wx_recv, wy_send, wy_recv,
    proj_sem, pj_send, pj_recv, pc_send, pc_recv, hd_send, hd_recv, ps_send, ps_recv, xz_send, xz_recv, xl_send, xl_recv,
    xs_send, xs_recv, hid_send, hid_recv, ret_send, ret_recv, rz_send, rz_recv,
):
    me = Place()
    s, z, l = me.s, me.z, me.l
    block = me.y * 2 + me.c

    group = pl.multiple_of(lax.div(z, 4) * HD, HD)
    loads = [
        pltpu.make_async_copy(src, dst, local_sem.at[k])
        for k, (src, dst) in enumerate(
            [
                (key_hbm.at[:, pl.ds(group, HD)], kv.at[me.yh, me.c, 0]),
                (val_hbm.at[:, pl.ds(group, HD)], kv.at[me.yh, me.c, 1]),
                (gain_hbm, gain_ref),
                (wg_hbm, wg),
                (wu_hbm, wu),
                (q_hbm, q_ref.at[0]),
                (res_hbm, res_ref),
                (ids_hbm, ids_ref),
                (score_hbm, score_ref),
            ]
        )
    ]
    for h in range(2):
        for c in range(2):
            dst = wdown.at[0, :, :, c, lax.rem(me.h + h, 2)]
            loads.append(pltpu.make_async_copy(wd_hbm.at[:, :, h, c], dst, local_sem.at[9 + 2 * h + c]))
    for cp in loads:
        cp.start()

    def proj_cols(at, half):
        return proj_hbm.at[:, pl.ds(pl.multiple_of(at * 256 + half * HD, HD), HD)]

    def proj_load(at):
        return pltpu.make_async_copy(
            proj_cols(at, l), proj.at[0, lax.div(at, 2), lax.rem(at, 2)], proj_sem.at[at]
        )

    def proj_stage(k):
        return pltpu.make_async_copy(proj_cols(2 * k + me.c, 1 - l), staged.at[k], proj_sem.at[NZ + k])

    proj_copy = remote(staged, proj.at[1, :, me.c], pj_send, pj_recv, me.at_other_l())

    def proj_load_start(at, _):
        proj_load(at).start()
        return 0

    def proj_stage_start(k, _):
        proj_stage(k).start()
        return 0

    lax.fori_loop(0, 8, proj_stage_start, 0)
    lax.fori_loop(0, NZ, proj_load_start, 0)

    def seq_peer(d):
        return (lax.rem(s + d, 16), me.e)

    def group_peer(d):
        other = lax.rem(block + lax.div(d, 2), 8)
        place = me.seq_of(lax.div(other, 2), me.h, lax.rem(other, 2))
        return (place, z * 2 + lax.rem(l + d, 2))

    barrier = pltpu.get_barrier_semaphore()

    def greet_seq(d, _):
        pl.semaphore_signal(barrier, inc=1, device_id=seq_peer(d), device_id_type=MESH)
        return 0

    def greet_group(d, _):
        pl.semaphore_signal(barrier, inc=1, device_id=group_peer(2 * d + 1), device_id_type=MESH)
        return 0

    lax.fori_loop(1, 16, greet_seq, 0)
    lax.fori_loop(0, 8, greet_group, 0)
    for k in (1, -1, 2, -2):
        pl.semaphore_signal(barrier, inc=1, device_id=me.at_z(k), device_id_type=MESH)

    loads[2].wait()
    loads[3].wait()
    loads[4].wait()
    gain = gain_ref[...]
    for at in range(NZ):
        cols = slice(at * 256, (at + 1) * 256)
        for i in range(2):
            wcat[at, 0, i, 0:64, :] = (wg[i, :, cols].astype(F32) * gain[:, cols]).astype(BF16)
            wcat[at, 0, i, 64:128, :] = (wu[i, :, cols].astype(F32) * gain[:, cols]).astype(BF16)

    loads[0].wait()
    loads[1].wait()
    pl.semaphore_wait(barrier, 15 + 8 + 4)

    def kv_copy(d):
        ref = kv.at[me.yh, me.c]
        target = lax.rem(me.yh + d, 8)
        return remote(ref, ref, kv_send.at[d], kv_recv.at[d], me.at_seq(target, me.c))

    q_copy = remote(q_hbm, q_ref.at[1], hd_send, hd_recv, me.at_other_l())
    q_copy.start()

    def kv_start(d, _):
        kv_copy(d).start()
        return 0

    lax.fori_loop(1, 8, kv_start, 0)

    def proj_staged(k, _):
        proj_stage(k).wait()
        return 0

    lax.fori_loop(0, 8, proj_staged, 0)
    proj_copy.start()
    def weight_copy(k):
        j, ab = lax.div(k, 2), lax.rem(k, 2)
        at = me.z_step(ab * (2 * j + 1) - j)
        return remote(
            wcat.at[at, 0], wcat.at[at, 1], wx_send.at[j, ab], wx_recv.at[j, ab], me.at_other_h()
        )

    def down_copy(h, c):
        dst = wdown.at[1, :, :, c, lax.rem(1 - me.h + h, 2)]
        k = 2 * h + c
        return remote(wd_hbm.at[:, :, h, c], dst, wy_send.at[k], wy_recv.at[k], me.at_other_h())


    for k in (7, 8):
        loads[k].wait()
    lane = lax.broadcasted_iota(jnp.int32, (128, ROWS), 1)
    slot = lax.broadcasted_iota(jnp.int32, (128, ROWS), 0)
    ids = ids_ref[...]
    weight = score_ref[...] / jnp.sum(score_ref[...], axis=0, keepdims=True)
    routed = jnp.zeros((128, ROWS), F32)
    shares = jnp.zeros((128, ROWS), F32)
    for q in range(4):
        pair = l if q < 2 else 1 - l
        match = ids == 4 * z + 2 * pair + q % 2
        here = lax.div(slot, CAP) == q
        routed = jnp.where(here, jnp.sum(jnp.where(match, 1.0, 0.0), axis=0, keepdims=True), routed)
        shares = jnp.where(here, jnp.sum(jnp.where(match, weight, 0.0), axis=0, keepdims=True), shares)
    earlier = jnp.where(slot < lane, 1.0, 0.0).astype(BF16)
    rank = dot(routed.astype(BF16), earlier)
    chosen = (routed > 0.5) & (rank == lax.rem(slot, CAP).astype(F32))
    table[...] = jnp.where(chosen, 1.0, 0.0).astype(BF16)
    spread_all = jnp.where(chosen, shares, 0.0).T
    spread_high = spread_all.astype(BF16)
    spread[0] = spread_high
    spread[1] = (spread_all - spread_high.astype(F32)).astype(BF16)
    acc[...] = jnp.zeros_like(acc)
    ssq[...] = jnp.zeros_like(ssq)
    for cp in loads[5:7] + loads[9:]:
        cp.wait()

    def proj_loaded(at, _):
        proj_load(at).wait()
        return 0

    lax.fori_loop(0, NZ, proj_loaded, 0)

    def kv_wait(d, _):
        ref = kv.at[lax.rem(me.yh + 8 - d, 8), me.c]
        remote(ref, ref, kv_send.at[d], kv_recv.at[d], me.at_other_core()).wait_recv()
        return 0

    lax.fori_loop(1, 8, kv_wait, 0)
    ref = kv.at[:, me.c]
    core_copy = remote(ref, ref, core_send, core_recv, me.at_other_core())
    core_copy.start()

    proj_copy.wait_recv()
    ref = proj.at[1, :, me.c]
    proj_core = remote(ref, ref, pc_send, pc_recv, me.at_other_core())
    proj_core.start()

    weight_copy(jnp.int32(0)).start()
    weight_copy(jnp.int32(1)).start()
    ref = kv.at[:, 1 - me.c]
    remote(ref, ref, core_send, core_recv, me.at_other_core()).wait_recv()

    q_copy.wait_recv()
    keys = kv[:, :, 0].reshape(16 * ROWS, HD)
    values = kv[:, :, 1].reshape(16 * ROWS, HD)
    key_pos = lax.broadcasted_iota(jnp.int32, (ROWS, 16 * ROWS), 1)
    query_pos = lax.broadcasted_iota(jnp.int32, (ROWS, 16 * ROWS), 0) + s * ROWS
    for k in range(2):
        scores = dot_t(q_ref[k], keys) * HD ** (-0.5)
        scores = jnp.where(query_pos >= key_pos, scores, NEG_FILL)
        row_max = jnp.max(scores, axis=1, keepdims=True)
        exp_weights = jnp.exp(scores - row_max)
        row_total = jnp.sum(exp_weights, axis=1, keepdims=True)
        heads[k] = (dot(exp_weights.astype(BF16), values) / row_total).astype(BF16)
    ref = proj.at[1, :, 1 - me.c]
    remote(ref, ref, pc_send, pc_recv, me.at_other_core()).wait_recv()

    def head_share(target):
        at, odd = lax.div(target, 2), lax.rem(target, 2)
        return dot(heads[0], proj[0, at, odd]) + dot(heads[1], proj[1, at, odd])

    head_sum = ZSum(me, head_share, sum_in, sum_out, ps_send, ps_recv)
    projected = head_sum.run(lambda k: weight_copy(k + jnp.int32(2)).start())
    attn_ref[...] = projected.astype(BF16)
    xcols[z] = (projected + res_ref[...].astype(F32)).astype(BF16)
    x_ring = ZRing(me, xcols, xz_send, xz_recv)
    x_ring.start()

    xs_gather = GroupGather(me, xs, xs_send, xs_recv)

    def x_swap(j):
        return remote(
            sx.at[j],
            xs.at[j, me.y, me.c, :, :, pl.ds(pl.multiple_of(l * HD, HD), HD)],
            xl_send.at[j],
            xl_recv.at[j],
            me.at_other_l(),
        )

    def dispatch(t, _):
        @pl.when(t < STEPS)
        def _():
            low, high = x_ring.step(t)
            for ab, at in enumerate((low, high)):
                picked = dot(table[...], xcols[at]).astype(BF16)
                sx[t, ab] = picked[64:]
                xs[t, me.y, me.c, ab, :, pl.ds(pl.multiple_of(l * HD, HD), HD)] = picked[:64]
            x_swap(t).start()

            @pl.when(t < 6)
            def _():
                weight_copy(t + 10).start()

        @pl.when((t >= 1) & (t < STEPS + 1))
        def _():
            j = t - 1
            ref = xs.at[j, me.y, me.c, :, :, pl.ds(pl.multiple_of((1 - l) * HD, HD), HD)]
            remote(ref, ref, xl_send.at[j], xl_recv.at[j], me.at_other_l()).wait_recv()
            xs_gather.a(j)

        @pl.when((t >= 2) & (t < STEPS + 2))
        def _():
            xs_gather.d(t - 2)

        for h in range(2):
            for c in range(2):

                @pl.when(t == 6 + 2 * h + c)
                def _():
                    down_copy(h, c).start()

        @pl.when(t >= 3)
        def _():
            j = t - 3
            xs_gather.e(j)
            for ab in range(2):
                at = me.z_step(j + 1) if ab else me.z_step(-j)
                ref = wcat.at[at, 1]
                remote(ref, ref, wx_send.at[j, ab], wx_recv.at[j, ab], me.at_other_h()).wait_recv()
                for i in range(2):
                    x = xs[j, :, :, ab, pl.ds(i * CAP, CAP), :].reshape(8 * CAP, 256)
                    for own in range(2):
                        acc[i, own] += dot_t(x, wcat[at, own, i])
                    wide = x.astype(F32)
                    square = wide * wide
                    ssq[i] += square[:, :128] + square[:, 128:]

        return 0

    lax.fori_loop(0, STEPS + 3, dispatch, 0)

    hid_gather = GroupGather(me, hid, hid_send, hid_recv)
    for k in range(CHUNKS):
        i = k % 2
        rows = pl.ds((k // 2) * ROWS, ROWS)
        scale = lax.rsqrt(jnp.sum(ssq[i, rows, :], axis=1, keepdims=True) * (1.0 / D) + NORM_EPS)
        made = []
        for own in range(2):
            gate = acc[i, own, rows, 0:64] * scale
            up = acc[i, own, rows, 64:128] * scale
            made.append((gate / (1.0 + jnp.exp(-gate)) * up).astype(BF16))
        hid[k, me.y, me.c] = jnp.concatenate(made, axis=1).reshape(2, HALF, 128)
        hid_gather.a(k)

    def down_ready(h, c):
        dst = wdown.at[1, :, :, c, lax.rem(me.h + h, 2)]
        k = 2 * h + c
        remote(dst, dst, wy_send.at[k], wy_recv.at[k], me.at_other_h()).wait_recv()

    def down(k):
        i = k % 2
        totals = [jnp.zeros((ROWS, 256), F32)] * 2
        for y in range(4):
            for c in range(2):
                rows = hid[k, y, c].reshape(ROWS, 128)
                for side in range(2):
                    totals[side] += dot(rows, wdown[side, i, y, c].reshape(128, 256))
        blocks = pl.ds((k // 2) * 4, 4)
        for side in range(2):
            for half in range(2):
                made = totals[side][:, half * HD:(half + 1) * HD].astype(BF16)
                prod[blocks, half, pl.ds(i * CAP, CAP), side * HD:(side + 1) * HD] = made.reshape(4, CAP, HD)

    def back_copy(d):
        other = lax.rem(block + lax.div(d, 2), 8)
        odd = lax.rem(d, 2)
        return remote(
            prod.at[other, lax.rem(l + d, 2)],
            ret.at[block, pl.ds(pl.multiple_of(odd * 64, 64), 64), :],
            ret_send.at[d],
            ret_recv.at[d],
            group_peer(d),
        )

    def back_start(target, _):
        for odd in range(2):
            d = 2 * lax.rem(target + 8 - block, 8) + odd

            @pl.when(d != 0)
            def _():
                back_copy(d).start()

        return 0

    for t in range(CHUNKS + 1):
        if t < CHUNKS:
            hid_gather.d(t)
        if t >= 1:
            hid_gather.e(t - 1)
            if t == 1:
                for h in range(2):
                    for c in range(2):
                        down_ready(h, c)
            down(t - 1)
            if t == 2:
                lax.fori_loop(0, 4, back_start, 0)
            if t == 4:
                lax.fori_loop(4, 8, back_start, 0)

    ret[block, 0:64, :] = prod[block, l]

    def back_wait(d, _):
        odd = lax.rem(d, 2)
        other = lax.rem(block + 8 - lax.div(d, 2), 8)
        ref = ret.at[other, pl.ds(pl.multiple_of(odd * 64, 64), 64), :]
        remote(ref, ref, ret_send.at[d], ret_recv.at[d], me.at_other_l()).wait_recv()
        return 0

    lax.fori_loop(1, 16, back_wait, 0)

    def expert_share(target):
        at = lax.div(target, 4) * 2 + lax.rem(target, 2)
        side = lax.rem(lax.div(target, 2) + me.h, 2)
        returned = ret[at, :, pl.ds(pl.multiple_of(side * HD, HD), HD)]
        return dot(spread[0], returned) + dot(spread[1], returned)

    expert_sum = ZSum(me, expert_share, ring_in, ring_out, rz_send, rz_recv)
    out_ref[...] = expert_sum.run().astype(BF16)

    core_copy.wait_send()
    head_sum.finish()
    x_ring.finish()
    expert_sum.finish()
    proj_core.wait_send()
    q_copy.wait_send()
    for h in range(2):
        for c in range(2):
            down_copy(h, c).wait_send()

    def kv_sent(d, _):
        kv_copy(d).wait_send()
        return 0

    proj_copy.wait_send()

    def back_sent(d, _):
        back_copy(d).wait_send()
        return 0

    def xs_sent(j, _):
        x_swap(j).wait_send()
        xs_gather.finish(j)
        weight_copy(2 * j).wait_send()
        weight_copy(2 * j + 1).wait_send()
        return 0

    def hid_sent(j, _):
        hid_gather.finish(j)
        return 0

    lax.fori_loop(1, 8, kv_sent, 0)
    lax.fori_loop(1, 16, back_sent, 0)
    lax.fori_loop(0, STEPS, xs_sent, 0)
    lax.fori_loop(0, CHUNKS, hid_sent, 0)


def per_device(
    queries, key_states, value_states, residual, out_proj, norm_gain,
    expert_ids, gate_scores, w_gate, w_up, w_down,
):
    vmem = pl.BlockSpec(memory_space=pltpu.VMEM)
    hbm = pl.BlockSpec(memory_space=pltpu.MemorySpace.HBM)
    dma = pltpu.SemaphoreType.DMA
    out = jax.ShapeDtypeStruct((ROWS, HD), BF16)
    scratch = [
        pltpu.VMEM((2, ROWS, HD), BF16),
        pltpu.VMEM((ROWS, HD), BF16),
        pltpu.VMEM((1, D), F32),
        pltpu.VMEM((8, ROWS), jnp.int32),
        pltpu.VMEM((8, ROWS), F32),
        pltpu.VMEM((8, 2, 2, ROWS, HD), BF16),
        pltpu.VMEM((2, 8, 2, HD, HD), BF16),
        pltpu.VMEM((8, HD, HD), BF16),
        pltpu.VMEM((2, ROWS, HD), BF16),
        pltpu.VMEM((NZ, ROWS, HD), BF16),
        pltpu.VMEM((STEPS, 4, 2, 2, 64, 256), BF16),
        pltpu.VMEM((STEPS, 2, 64, HD), BF16),
        pltpu.VMEM((2, 64, D), BF16),
        pltpu.VMEM((2, 64, D), BF16),
        pltpu.VMEM((NZ, 2, 2, 128, 256), BF16),
        pltpu.VMEM((2, 2, 4, 2, 2, 64, 256), BF16),
        pltpu.VMEM((2, 2, 256, 128), F32),
        pltpu.VMEM((2, 256, 128), F32),
        pltpu.VMEM((CHUNKS, 4, 2, 2, HALF, 128), BF16),
        pltpu.VMEM((8, 2, 64, 256), BF16),
        pltpu.VMEM((8, 128, 256), BF16),
        pltpu.VMEM((128, ROWS), BF16),
        pltpu.VMEM((2, ROWS, 128), BF16),
        pltpu.VMEM((2, 9, ROWS, HD), BF16),
        pltpu.VMEM((2, 9, ROWS, HD), BF16),
        pltpu.VMEM((2, 9, ROWS, HD), BF16),
        pltpu.VMEM((2, 9, ROWS, HD), BF16),
        dma((13,)),
        dma((8,)), dma((8,)),
        dma, dma,
        dma((STEPS, 2)), dma((STEPS, 2)),
        dma((4,)), dma((4,)),
        dma((NZ + 8,)),
        dma, dma,
        dma, dma,
        dma, dma,
        dma((2, 9)), dma((2, 9)),
        dma((2, 9)), dma((2, 9)),
        dma((STEPS,)), dma((STEPS,)),
        dma((STEPS, 4)), dma((STEPS, 4)),
        dma((CHUNKS, 4)), dma((CHUNKS, 4)),
        dma((16,)), dma((16,)),
        dma((2, 9)), dma((2, 9)),
    ]
    return pl.pallas_call(
        kernel,
        out_shape=(out, out),
        in_specs=[hbm] * 11,
        out_specs=(vmem, vmem),
        scratch_shapes=scratch,
        compiler_params=pltpu.CompilerParams(
            collective_id=0, has_side_effects=True, vmem_limit_bytes=63 * 2**20
        ),
        cost_estimate=pl.CostEstimate(flops=2 * 10**9, bytes_accessed=8 * 10**6, transcendentals=10**6),
        name="layer",
    )(
        queries, residual, norm_gain.reshape(1, D), expert_ids.T, gate_scores.T,
        key_states, value_states, out_proj, w_gate, w_up,
        w_down.reshape(2, 4, 2, 2, 64, 256),
    )


def solution(mesh):
    placed = (
        P("seq", "exp"),
        P("seq", None),
        P("seq", None),
        P("seq", "exp"),
        P("exp", None),
        P(),
        P("seq", None),
        P("seq", None),
        P("exp", "seq", None),
        P("exp", "seq", None),
        P("exp", None, "seq"),
    )
    return jax.shard_map(
        per_device,
        mesh=mesh,
        in_specs=placed,
        out_specs=(P("seq", "exp"), P("seq", "exp")),
        check_vma=False,
    )
```

```python
import jax
import jax.numpy as jnp
from jax import lax
from jax.experimental import pallas as pl
from jax.experimental.pallas import tpu as pltpu
from jax.sharding import PartitionSpec as P

MESH = pl.DeviceIdType.MESH
BF16 = jnp.bfloat16
F32 = jnp.float32
NEG_FILL = -1e30
NORM_EPS = 1e-06
D = 4096
HD = 128
ROWS = 128
NZ = 16
STEPS = 8
CAP = 32
CHUNKS = 4
HALF = 64


def dot(a, b):
    return jnp.dot(a, b, preferred_element_type=F32)


def dot_t(a, b):
    return lax.dot_general(a, b, (((1,), (1,)), ((), ())), preferred_element_type=F32)


def remote(src, dst, send_sem, recv_sem, device):
    return pltpu.make_async_remote_copy(
        src_ref=src,
        dst_ref=dst,
        send_sem=send_sem,
        recv_sem=recv_sem,
        device_id=device,
        device_id_type=MESH,
    )


class Place:
    def __init__(self):
        self.s = lax.axis_index("seq")
        self.e = lax.axis_index("exp")
        self.yh = lax.div(self.s, 2)
        self.c = lax.rem(self.s, 2)
        self.y = lax.div(self.s, 4)
        self.h = lax.rem(self.yh, 2)
        self.z = lax.div(self.e, 2)
        self.l = lax.rem(self.e, 2)

    def seq_of(self, y, h, c):
        return (y * 2 + h) * 2 + c

    def y_step(self, k):
        return lax.rem(self.y + k + 4, 4)

    def z_step(self, k):
        return lax.rem(self.z + k + 32, NZ)

    def at_seq(self, yh, c):
        return (yh * 2 + c, self.e)

    def at_y(self, k):
        return (self.seq_of(self.y_step(k), self.h, self.c), self.e)

    def at_other_h(self):
        return (self.seq_of(self.y, 1 - self.h, self.c), self.e)

    def at_other_core(self):
        return (self.seq_of(self.y, self.h, 1 - self.c), self.e)

    def at_z(self, k):
        return (self.s, self.z_step(k) * 2 + self.l)

    def at_other_l(self):
        return (self.s, self.z * 2 + 1 - self.l)


class GroupGather:
    def __init__(self, me, buf, send, recv):
        self.me, self.buf, self.send, self.recv = me, buf, send, recv

    def copy(self, j, k, ref, device):
        return remote(ref, ref, self.send.at[j, k], self.recv.at[j, k], device)

    def push(self, j, k):
        me = self.me
        if k < 3:
            return self.copy(j, k, self.buf.at[j, me.y, me.c], me.at_y((1, -1, 2)[k]))
        return self.copy(j, k, self.buf.at[j, :, me.c], me.at_other_core())

    def arrived(self, j, k):
        me = self.me
        if k < 3:
            ref = self.buf.at[j, me.y_step((-1, 1, 2)[k]), me.c]
        else:
            ref = self.buf.at[j, :, 1 - me.c]
        self.copy(j, k, ref, me.at_other_core()).wait_recv()

    def a(self, j):
        for k in (2, 0, 1):
            self.push(j, k).start()

    def d(self, j):
        for k in range(3):
            self.arrived(j, k)
        self.push(j, 3).start()

    def e(self, j):
        self.arrived(j, 3)

    def finish(self, j):
        for k in range(4):
            self.push(j, k).wait_send()


class ZRing:
    def __init__(self, me, buf, send, recv):
        self.me, self.buf, self.send, self.recv = me, buf, send, recv

    def copy(self, way, k, block, hops):
        ref = self.buf.at[block]
        return remote(
            ref, ref, self.send.at[way, k], self.recv.at[way, k], self.me.at_z(hops - 2 * way * hops)
        )

    def up(self, k, hops=2):
        return self.copy(0, k, self.me.z_step(hops - k), hops)

    def down(self, k, hops=2):
        return self.copy(1, k, self.me.z_step(k - hops), hops)

    def start(self):
        for hops in (1, 2):
            self.down(hops, hops).start()
            self.up(hops, hops).start()

    def step(self, j):
        low, high = self.me.z_step(-j), self.me.z_step(j + 1)
        self.copy(1, j + 1, high, 2).wait_recv()

        @pl.when(j < STEPS - 2)
        def _():
            self.down(j + 3).start()

        @pl.when(j >= 1)
        def _():
            self.copy(0, j, low, 2).wait_recv()

            @pl.when(j < STEPS - 2)
            def _():
                self.up(j + 2).start()

        return low, high

    def finish(self):
        for hops in (1, 2):
            self.down(hops, hops).wait_send()
            self.up(hops, hops).wait_send()

        def one(k, _):
            self.down(k).wait_send()

            @pl.when(k < STEPS)
            def _():
                self.up(k).wait_send()

            return 0

        lax.fori_loop(3, STEPS + 1, one, 0)


class ZSum:
    def __init__(self, me, share, inbox, outbox, send, recv):
        self.me, self.share = me, share
        self.inbox, self.outbox, self.send, self.recv = inbox, outbox, send, recv

    def copy(self, way, k, hops=2):
        return remote(
            self.outbox.at[way, k],
            self.inbox.at[way, k],
            self.send.at[way, k],
            self.recv.at[way, k],
            self.me.at_z(hops - 2 * way * hops),
        )

    def step(self, k, beside, first=False, hops=(2, 2)):
        places = [(0, 8 - k, self.me.z_step(8 - k))]
        if len(hops) > 1:
            places.append((1, 7 - k, self.me.z_step(k - 7)))
        shares = [self.share(target) for _, _, target in places]
        for (way, far, _), part in zip(places, shares):
            if not first:
                self.copy(way, far + 2).wait_recv()
                part = part + self.inbox[way, far + 2].astype(F32)
            self.outbox[way, far] = part.astype(BF16)
            self.copy(way, far, hops[way]).start()
        beside(k)

    def run(self, beside=lambda k: None):
        self.step(0, beside, first=True)
        self.step(1, beside, first=True)

        def one(k, _):
            self.step(k, beside)
            return 0

        lax.fori_loop(2, 6, one, 0)
        self.step(6, beside, hops=(2, 1))
        self.step(7, beside, hops=(1,))
        total = self.share(self.me.z)
        for k in (2, 1):
            for way in (1, 0):
                self.copy(way, k).wait_recv()
                total = total + self.inbox[way, k].astype(F32)
        return total

    def finish(self):
        def one(k, _):
            self.copy(0, k).wait_send()

            @pl.when(k < 8)
            def _():
                self.copy(1, k).wait_send()

            return 0

        lax.fori_loop(1, 9, one, 0)


def kernel(
    q_hbm, res_hbm, gain_hbm, ids_hbm, score_hbm,
    key_hbm, val_hbm, proj_hbm, wg_hbm, wu_hbm, wd_hbm,
    attn_ref, out_ref,
    q_ref, res_ref, gain_ref, ids_ref, score_ref,
    kv, proj, staged, heads, xcols, xs, sx,
    wg, wu, wcat, wdown, acc, ssq, hid, prod, ret, table, spread,
    sum_in, sum_out, ring_in, ring_out,
    local_sem, kv_send, kv_recv, core_send, core_recv, wx_send, wx_recv, wy_send, wy_recv,
    proj_sem, pj_send, pj_recv, pc_send, pc_recv, hd_send, hd_recv, ps_send, ps_recv, xz_send, xz_recv, xl_send, xl_recv,
    xs_send, xs_recv, hid_send, hid_recv, ret_send, ret_recv, rz_send, rz_recv,
):
    me = Place()
    s, z, l = me.s, me.z, me.l
    block = me.y * 2 + me.c

    group = pl.multiple_of(lax.div(z, 4) * HD, HD)
    loads = [
        pltpu.make_async_copy(src, dst, local_sem.at[k])
        for k, (src, dst) in enumerate(
            [
                (key_hbm.at[:, pl.ds(group, HD)], kv.at[me.yh, me.c, 0]),
                (val_hbm.at[:, pl.ds(group, HD)], kv.at[me.yh, me.c, 1]),
                (gain_hbm, gain_ref),
                (wg_hbm, wg),
                (wu_hbm, wu),
                (q_hbm, q_ref.at[0]),
                (res_hbm, res_ref),
                (ids_hbm, ids_ref),
                (score_hbm, score_ref),
            ]
        )
    ]
    for h in range(2):
        for c in range(2):
            dst = wdown.at[0, :, :, c, lax.rem(me.h + h, 2)]
            loads.append(pltpu.make_async_copy(wd_hbm.at[:, :, h, c], dst, local_sem.at[9 + 2 * h + c]))
    for cp in loads:
        cp.start()

    def proj_cols(at, half):
        return proj_hbm.at[:, pl.ds(pl.multiple_of(at * 256 + half * HD, HD), HD)]

    def proj_load(at):
        return pltpu.make_async_copy(
            proj_cols(at, l), proj.at[0, lax.div(at, 2), lax.rem(at, 2)], proj_sem.at[at]
        )

    def proj_stage(k):
        return pltpu.make_async_copy(proj_cols(2 * k + me.c, 1 - l), staged.at[k], proj_sem.at[NZ + k])

    proj_copy = remote(staged, proj.at[1, :, me.c], pj_send, pj_recv, me.at_other_l())

    def proj_load_start(at, _):
        proj_load(at).start()
        return 0

    def proj_stage_start(k, _):
        proj_stage(k).start()
        return 0

    lax.fori_loop(0, 8, proj_stage_start, 0)
    lax.fori_loop(0, NZ, proj_load_start, 0)

    def seq_peer(d):
        return (lax.rem(s + d, 16), me.e)

    def group_peer(d):
        other = lax.rem(block + lax.div(d, 2), 8)
        place = me.seq_of(lax.div(other, 2), me.h, lax.rem(other, 2))
        return (place, z * 2 + lax.rem(l + d, 2))

    barrier = pltpu.get_barrier_semaphore()

    def greet_seq(d, _):
        pl.semaphore_signal(barrier, inc=1, device_id=seq_peer(d), device_id_type=MESH)
        return 0

    def greet_group(d, _):
        pl.semaphore_signal(barrier, inc=1, device_id=group_peer(2 * d + 1), device_id_type=MESH)
        return 0

    lax.fori_loop(1, 16, greet_seq, 0)
    lax.fori_loop(0, 8, greet_group, 0)
    for k in (1, -1, 2, -2):
        pl.semaphore_signal(barrier, inc=1, device_id=me.at_z(k), device_id_type=MESH)

    loads[2].wait()
    loads[3].wait()
    loads[4].wait()
    gain = gain_ref[...]
    for at in range(NZ):
        cols = slice(at * 256, (at + 1) * 256)
        for i in range(2):
            wcat[at, 0, i, 0:64, :] = (wg[i, :, cols].astype(F32) * gain[:, cols]).astype(BF16)
            wcat[at, 0, i, 64:128, :] = (wu[i, :, cols].astype(F32) * gain[:, cols]).astype(BF16)

    loads[0].wait()
    loads[1].wait()
    pl.semaphore_wait(barrier, 15 + 8 + 4)

    def kv_copy(d):
        ref = kv.at[me.yh, me.c]
        target = lax.rem(me.yh + d, 8)
        return remote(ref, ref, kv_send.at[d], kv_recv.at[d], me.at_seq(target, me.c))

    q_copy = remote(q_hbm, q_ref.at[1], hd_send, hd_recv, me.at_other_l())
    q_copy.start()

    def kv_start(d, _):
        kv_copy(d).start()
        return 0

    lax.fori_loop(1, 8, kv_start, 0)

    def proj_staged(k, _):
        proj_stage(k).wait()
        return 0

    lax.fori_loop(0, 8, proj_staged, 0)
    proj_copy.start()
    def weight_copy(k):
        j, ab = lax.div(k, 2), lax.rem(k, 2)
        at = me.z_step(ab * (2 * j + 1) - j)
        return remote(
            wcat.at[at, 0], wcat.at[at, 1], wx_send.at[j, ab], wx_recv.at[j, ab], me.at_other_h()
        )

    def down_copy(h, c):
        dst = wdown.at[1, :, :, c, lax.rem(1 - me.h + h, 2)]
        k = 2 * h + c
        return remote(wd_hbm.at[:, :, h, c], dst, wy_send.at[k], wy_recv.at[k], me.at_other_h())


    for k in (7, 8):
        loads[k].wait()
    lane = lax.broadcasted_iota(jnp.int32, (128, ROWS), 1)
    slot = lax.broadcasted_iota(jnp.int32, (128, ROWS), 0)
    ids = ids_ref[...]
    weight = score_ref[...] / jnp.sum(score_ref[...], axis=0, keepdims=True)
    routed = jnp.zeros((128, ROWS), F32)
    shares = jnp.zeros((128, ROWS), F32)
    for q in range(4):
        pair = l if q < 2 else 1 - l
        match = ids == 4 * z + 2 * pair + q % 2
        here = lax.div(slot, CAP) == q
        routed = jnp.where(here, jnp.sum(jnp.where(match, 1.0, 0.0), axis=0, keepdims=True), routed)
        shares = jnp.where(here, jnp.sum(jnp.where(match, weight, 0.0), axis=0, keepdims=True), shares)
    earlier = jnp.where(slot < lane, 1.0, 0.0).astype(BF16)
    rank = dot(routed.astype(BF16), earlier)
    chosen = (routed > 0.5) & (rank == lax.rem(slot, CAP).astype(F32))
    table[...] = jnp.where(chosen, 1.0, 0.0).astype(BF16)
    spread_all = jnp.where(chosen, shares, 0.0).T
    spread_high = spread_all.astype(BF16)
    spread[0] = spread_high
    spread[1] = (spread_all - spread_high.astype(F32)).astype(BF16)
    acc[...] = jnp.zeros_like(acc)
    ssq[...] = jnp.zeros_like(ssq)
    for cp in loads[5:7] + loads[9:]:
        cp.wait()

    def proj_loaded(at, _):
        proj_load(at).wait()
        return 0

    lax.fori_loop(0, NZ, proj_loaded, 0)

    def kv_wait(d, _):
        ref = kv.at[lax.rem(me.yh + 8 - d, 8), me.c]
        remote(ref, ref, kv_send.at[d], kv_recv.at[d], me.at_other_core()).wait_recv()
        return 0

    lax.fori_loop(1, 8, kv_wait, 0)
    ref = kv.at[:, me.c]
    core_copy = remote(ref, ref, core_send, core_recv, me.at_other_core())
    core_copy.start()

    proj_copy.wait_recv()
    ref = proj.at[1, :, me.c]
    proj_core = remote(ref, ref, pc_send, pc_recv, me.at_other_core())
    proj_core.start()

    weight_copy(jnp.int32(0)).start()
    weight_copy(jnp.int32(1)).start()
    ref = kv.at[:, 1 - me.c]
    remote(ref, ref, core_send, core_recv, me.at_other_core()).wait_recv()

    q_copy.wait_recv()
    keys = kv[:, :, 0].reshape(16 * ROWS, HD)
    values = kv[:, :, 1].reshape(16 * ROWS, HD)
    key_pos = lax.broadcasted_iota(jnp.int32, (ROWS, 16 * ROWS), 1)
    query_pos = lax.broadcasted_iota(jnp.int32, (ROWS, 16 * ROWS), 0) + s * ROWS
    for k in range(2):
        scores = dot_t(q_ref[k], keys) * HD ** (-0.5)
        scores = jnp.where(query_pos >= key_pos, scores, NEG_FILL)
        row_max = jnp.max(scores, axis=1, keepdims=True)
        exp_weights = jnp.exp(scores - row_max)
        row_total = jnp.sum(exp_weights, axis=1, keepdims=True)
        heads[k] = (dot(exp_weights.astype(BF16), values) / row_total).astype(BF16)
    ref = proj.at[1, :, 1 - me.c]
    remote(ref, ref, pc_send, pc_recv, me.at_other_core()).wait_recv()

    def head_share(target):
        at, odd = lax.div(target, 2), lax.rem(target, 2)
        return dot(heads[0], proj[0, at, odd]) + dot(heads[1], proj[1, at, odd])

    head_sum = ZSum(me, head_share, sum_in, sum_out, ps_send, ps_recv)
    projected = head_sum.run(lambda k: weight_copy(k + jnp.int32(2)).start())
    attn_ref[...] = projected.astype(BF16)
    xcols[z] = (projected + res_ref[...].astype(F32)).astype(BF16)
    x_ring = ZRing(me, xcols, xz_send, xz_recv)
    x_ring.start()

    xs_gather = GroupGather(me, xs, xs_send, xs_recv)

    def x_swap(j):
        return remote(
            sx.at[j],
            xs.at[j, me.y, me.c, :, :, pl.ds(pl.multiple_of(l * HD, HD), HD)],
            xl_send.at[j],
            xl_recv.at[j],
            me.at_other_l(),
        )

    def dispatch(t, _):
        @pl.when(t < STEPS)
        def _():
            low, high = x_ring.step(t)
            for ab, at in enumerate((low, high)):
                picked = dot(table[...], xcols[at]).astype(BF16)
                sx[t, ab] = picked[64:]
                xs[t, me.y, me.c, ab, :, pl.ds(pl.multiple_of(l * HD, HD), HD)] = picked[:64]
            x_swap(t).start()

            @pl.when(t < 6)
            def _():
                weight_copy(t + 10).start()

        @pl.when((t >= 1) & (t < STEPS + 1))
        def _():
            j = t - 1
            ref = xs.at[j, me.y, me.c, :, :, pl.ds(pl.multiple_of((1 - l) * HD, HD), HD)]
            remote(ref, ref, xl_send.at[j], xl_recv.at[j], me.at_other_l()).wait_recv()
            xs_gather.a(j)

        @pl.when((t >= 2) & (t < STEPS + 2))
        def _():
            xs_gather.d(t - 2)

        for h in range(2):
            for c in range(2):

                @pl.when(t == 6 + 2 * h + c)
                def _():
                    down_copy(h, c).start()

        @pl.when(t >= 3)
        def _():
            j = t - 3
            xs_gather.e(j)
            for ab in range(2):
                at = me.z_step(j + 1) if ab else me.z_step(-j)
                ref = wcat.at[at, 1]
                remote(ref, ref, wx_send.at[j, ab], wx_recv.at[j, ab], me.at_other_h()).wait_recv()
                for i in range(2):
                    x = xs[j, :, :, ab, pl.ds(i * CAP, CAP), :].reshape(8 * CAP, 256)
                    for own in range(2):
                        acc[i, own] += dot_t(x, wcat[at, own, i])
                    wide = x.astype(F32)
                    square = wide * wide
                    ssq[i] += square[:, :128] + square[:, 128:]

        return 0

    lax.fori_loop(0, STEPS + 3, dispatch, 0)

    hid_gather = GroupGather(me, hid, hid_send, hid_recv)
    for k in range(CHUNKS):
        i = k % 2
        rows = pl.ds((k // 2) * ROWS, ROWS)
        scale = lax.rsqrt(jnp.sum(ssq[i, rows, :], axis=1, keepdims=True) * (1.0 / D) + NORM_EPS)
        made = []
        for own in range(2):
            gate = acc[i, own, rows, 0:64] * scale
            up = acc[i, own, rows, 64:128] * scale
            made.append((gate / (1.0 + jnp.exp(-gate)) * up).astype(BF16))
        hid[k, me.y, me.c] = jnp.concatenate(made, axis=1).reshape(2, HALF, 128)
        hid_gather.a(k)

    def down_ready(h, c):
        dst = wdown.at[1, :, :, c, lax.rem(me.h + h, 2)]
        k = 2 * h + c
        remote(dst, dst, wy_send.at[k], wy_recv.at[k], me.at_other_h()).wait_recv()

    def down(k):
        i = k % 2
        totals = [jnp.zeros((ROWS, 256), F32)] * 2
        for y in range(4):
            for c in range(2):
                rows = hid[k, y, c].reshape(ROWS, 128)
                for side in range(2):
                    totals[side] += dot(rows, wdown[side, i, y, c].reshape(128, 256))
        blocks = pl.ds((k // 2) * 4, 4)
        for side in range(2):
            for half in range(2):
                made = totals[side][:, half * HD:(half + 1) * HD].astype(BF16)
                prod[blocks, half, pl.ds(i * CAP, CAP), side * HD:(side + 1) * HD] = made.reshape(4, CAP, HD)

    def back_copy(d):
        other = lax.rem(block + lax.div(d, 2), 8)
        odd = lax.rem(d, 2)
        return remote(
            prod.at[other, lax.rem(l + d, 2)],
            ret.at[block, pl.ds(pl.multiple_of(odd * 64, 64), 64), :],
            ret_send.at[d],
            ret_recv.at[d],
            group_peer(d),
        )

    def back_start(target, _):
        for odd in range(2):
            d = 2 * lax.rem(target + 8 - block, 8) + odd

            @pl.when(d != 0)
            def _():
                back_copy(d).start()

        return 0

    for t in range(CHUNKS + 1):
        if t < CHUNKS:
            hid_gather.d(t)
        if t >= 1:
            hid_gather.e(t - 1)
            if t == 1:
                for h in range(2):
                    for c in range(2):
                        down_ready(h, c)
            down(t - 1)
            if t == 2:
                lax.fori_loop(0, 4, back_start, 0)
            if t == 4:
                lax.fori_loop(4, 8, back_start, 0)

    ret[block, 0:64, :] = prod[block, l]

    def back_wait(d, _):
        odd = lax.rem(d, 2)
        other = lax.rem(block + 8 - lax.div(d, 2), 8)
        ref = ret.at[other, pl.ds(pl.multiple_of(odd * 64, 64), 64), :]
        remote(ref, ref, ret_send.at[d], ret_recv.at[d], me.at_other_l()).wait_recv()
        return 0

    core_copy.wait_send()
    head_sum.finish()
    x_ring.finish()
    proj_core.wait_send()
    q_copy.wait_send()
    for h in range(2):
        for c in range(2):
            down_copy(h, c).wait_send()

    def kv_sent(d, _):
        kv_copy(d).wait_send()
        return 0

    proj_copy.wait_send()

    def xs_sent(j, _):
        x_swap(j).wait_send()
        xs_gather.finish(j)
        weight_copy(2 * j).wait_send()
        weight_copy(2 * j + 1).wait_send()
        return 0

    def hid_sent(j, _):
        hid_gather.finish(j)
        return 0

    lax.fori_loop(1, 8, kv_sent, 0)
    lax.fori_loop(0, STEPS, xs_sent, 0)
    lax.fori_loop(0, CHUNKS, hid_sent, 0)

    lax.fori_loop(1, 16, back_wait, 0)

    def expert_share(target):
        at = lax.div(target, 4) * 2 + lax.rem(target, 2)
        side = lax.rem(lax.div(target, 2) + me.h, 2)
        returned = ret[at, :, pl.ds(pl.multiple_of(side * HD, HD), HD)]
        return dot(spread[0], returned) + dot(spread[1], returned)

    expert_sum = ZSum(me, expert_share, ring_in, ring_out, rz_send, rz_recv)
    out_ref[...] = expert_sum.run().astype(BF16)

    expert_sum.finish()

    def back_sent(d, _):
        back_copy(d).wait_send()
        return 0

    lax.fori_loop(1, 16, back_sent, 0)


def per_device(
    queries, key_states, value_states, residual, out_proj, norm_gain,
    expert_ids, gate_scores, w_gate, w_up, w_down,
):
    vmem = pl.BlockSpec(memory_space=pltpu.VMEM)
    hbm = pl.BlockSpec(memory_space=pltpu.MemorySpace.HBM)
    dma = pltpu.SemaphoreType.DMA
    out = jax.ShapeDtypeStruct((ROWS, HD), BF16)
    scratch = [
        pltpu.VMEM((2, ROWS, HD), BF16),
        pltpu.VMEM((ROWS, HD), BF16),
        pltpu.VMEM((1, D), F32),
        pltpu.VMEM((8, ROWS), jnp.int32),
        pltpu.VMEM((8, ROWS), F32),
        pltpu.VMEM((8, 2, 2, ROWS, HD), BF16),
        pltpu.VMEM((2, 8, 2, HD, HD), BF16),
        pltpu.VMEM((8, HD, HD), BF16),
        pltpu.VMEM((2, ROWS, HD), BF16),
        pltpu.VMEM((NZ, ROWS, HD), BF16),
        pltpu.VMEM((STEPS, 4, 2, 2, 64, 256), BF16),
        pltpu.VMEM((STEPS, 2, 64, HD), BF16),
        pltpu.VMEM((2, 64, D), BF16),
        pltpu.VMEM((2, 64, D), BF16),
        pltpu.VMEM((NZ, 2, 2, 128, 256), BF16),
        pltpu.VMEM((2, 2, 4, 2, 2, 64, 256), BF16),
        pltpu.VMEM((2, 2, 256, 128), F32),
        pltpu.VMEM((2, 256, 128), F32),
        pltpu.VMEM((CHUNKS, 4, 2, 2, HALF, 128), BF16),
        pltpu.VMEM((8, 2, 64, 256), BF16),
        pltpu.VMEM((8, 128, 256), BF16),
        pltpu.VMEM((128, ROWS), BF16),
        pltpu.VMEM((2, ROWS, 128), BF16),
        pltpu.VMEM((2, 9, ROWS, HD), BF16),
        pltpu.VMEM((2, 9, ROWS, HD), BF16),
        pltpu.VMEM((2, 9, ROWS, HD), BF16),
        pltpu.VMEM((2, 9, ROWS, HD), BF16),
        dma((13,)),
        dma((8,)), dma((8,)),
        dma, dma,
        dma((STEPS, 2)), dma((STEPS, 2)),
        dma((4,)), dma((4,)),
        dma((NZ + 8,)),
        dma, dma,
        dma, dma,
        dma, dma,
        dma((2, 9)), dma((2, 9)),
        dma((2, 9)), dma((2, 9)),
        dma((STEPS,)), dma((STEPS,)),
        dma((STEPS, 4)), dma((STEPS, 4)),
        dma((CHUNKS, 4)), dma((CHUNKS, 4)),
        dma((16,)), dma((16,)),
        dma((2, 9)), dma((2, 9)),
    ]
    return pl.pallas_call(
        kernel,
        out_shape=(out, out),
        in_specs=[hbm] * 11,
        out_specs=(vmem, vmem),
        scratch_shapes=scratch,
        compiler_params=pltpu.CompilerParams(
            collective_id=0, has_side_effects=True, vmem_limit_bytes=63 * 2**20
        ),
        cost_estimate=pl.CostEstimate(flops=2 * 10**9, bytes_accessed=8 * 10**6, transcendentals=10**6),
        name="layer",
    )(
        queries, residual, norm_gain.reshape(1, D), expert_ids.T, gate_scores.T,
        key_states, value_states, out_proj, w_gate, w_up,
        w_down.reshape(2, 4, 2, 2, 64, 256),
    )


def solution(mesh):
    placed = (
        P("seq", "exp"),
        P("seq", None),
        P("seq", None),
        P("seq", "exp"),
        P("exp", None),
        P(),
        P("seq", None),
        P("seq", None),
        P("exp", "seq", None),
        P("exp", "seq", None),
        P("exp", None, "seq"),
    )
    return jax.shard_map(
        per_device,
        mesh=mesh,
        in_specs=placed,
        out_specs=(P("seq", "exp"), P("seq", "exp")),
        check_vma=False,
    )
```
